256 devices in a mesh: frame: 32 (over z_hi, x, core), head: 8 (over z_lo, y).
Axes of the slice: x: 4, y: 4, z: 8 (z_hi: 4, z_lo: 2; z = z_hi * 2 + z_lo), core: 2. Of those that a mesh axis runs over, the one named last changes fastest.
Arguments:
- activations: bfloat16 [64, 128, 4096], P('frame'), may hold values from -6 to 6
- w_query: bfloat16 [4096, 4096], P('frame', 'head'), may hold values from -0.09375 to 0.09375
- w_key: bfloat16 [4096, 4096], P('frame', 'head'), may hold values from -0.09375 to 0.09375
- w_value: bfloat16 [4096, 4096], P('frame', 'head'), may hold values from -0.09375 to 0.09375
- q_gain: float32 [128], replicated, may hold values from 0.1 to 1.9
- k_gain: float32 [128], replicated, may hold values from 0.1 to 1.9
- grad_attn: bfloat16 [64, 128, 4096], P('frame', None, 'head'), may hold values from -6 to 6
Outputs:
- grad_input: bfloat16 [64, 128, 4096], P('frame', None, 'head')
- grad_wq: float32 [4096, 4096], P('frame', 'head')
- grad_wk: float32 [4096, 4096], P('frame', 'head')
- grad_wv: float32 [4096, 4096], P('frame', 'head')
The draws below stay inside these ranges and needn't reach their ends.
All inputs are finite; a program needn't handle non-finite values.
Results may differ from the reference program's by a relative error of at most 0.018.
Values may be sent and summed in bfloat16 or wider, within the bound.
No kernel may reach another device: no remote copies, remote signals or barrier semaphores. Data moves between devices by JAX's collectives and lax.ppermute only.
A program may use at most 128 MiB of HBM per device.

```python
import math
import jax
import jax.numpy as jnp
from jax import lax

D = 4096
HEADS = 32
HD = 128
FR_DEV = 2
PATCHES = 128
FRAMES = 64
N_FRAME = 32


def shard_levels(own_key, extent, shards, least, top_value):
    level = 1.0
    for axis_at, shards_of in shards:
        heights = jax.random.uniform(jax.random.fold_in(jax.random.fold_in(own_key, 6), axis_at), (shards_of,), jnp.float32, least / len(shards), top_value / len(shards))
        level = level * jnp.repeat(jnp.exp(heights), extent[axis_at] // shards_of).reshape((-1,) + (1,) * (len(extent) - 1 - axis_at))
    return level


def scatter_about(stream_key, dims, spread, limit, pieces=(), kind=jnp.bfloat16):
    level = shard_levels(stream_key, dims, pieces, -0.22, 0.18) if pieces else 1.0
    result = jax.random.normal(stream_key, dims, jnp.float32) * spread * level
    return jnp.minimum(jnp.maximum(result, -limit), limit).astype(kind)


def setup_inputs(seed: int = 0) -> dict:
    key_list = jax.random.split(jax.random.key(seed), 8)
    return {
        "activations": scatter_about(key_list[0], (FRAMES, PATCHES, D), 1.0, 6.0, ((0, 32),)),
        "w_query": scatter_about(key_list[1], (D, D), D ** -0.5, 0.09375, ((0, 32), (1, 8))),
        "w_key": scatter_about(key_list[2], (D, D), D ** -0.5, 0.09375, ((0, 32), (1, 8))),
        "w_value": scatter_about(key_list[3], (D, D), D ** -0.5, 0.09375, ((0, 32), (1, 8))),
        "q_gain": jnp.clip(1.0 + 0.18 * jax.random.normal(key_list[4], (HD,), jnp.float32), 0.1, 1.9),
        "k_gain": jnp.clip(1.0 + 0.18 * jax.random.normal(key_list[5], (HD,), jnp.float32), 0.1, 1.9),
        "grad_attn": scatter_about(key_list[6], (FRAMES, PATCHES, D), 1.0, 6.0, ((0, 32), (2, 8))),
    }


epsilon = 1e-06

def scaled(raw, gain):
    inverse = lax.rsqrt(lax.optimization_barrier(jnp.mean(raw * raw, axis=-1, keepdims=True)) + epsilon)
    return raw * inverse * gain

def attend(query, key_norm, value):
    factor = 1.0 / math.sqrt(query.shape[-1])
    scores = jnp.einsum('fphd,gphd->phfg', query, key_norm) * factor
    expon = jnp.exp(scores)
    weights = expon / lax.optimization_barrier(jnp.sum(expon, axis=-1, keepdims=True))
    return jnp.einsum('phfg,gphd->fphd', weights, value)

def attend_back(query, key_norm, value, cotan):
    _, pull = jax.vjp(attend, query.astype(jnp.float32), key_norm.astype(jnp.float32), value.astype(jnp.float32))
    grads = pull(cotan.astype(jnp.float32))
    return (grads[0].astype(jnp.bfloat16), grads[1].astype(jnp.bfloat16), grads[2].astype(jnp.bfloat16))

def reference(activations, w_query, w_key, w_value, q_gain, k_gain, grad_attn):
    head_dim = D // HEADS
    shape4 = (FRAMES, PATCHES, HEADS, head_dim)
    tok_rows = activations.reshape(FRAMES * PATCHES, D)
    q_raw = jnp.dot(tok_rows, w_query, preferred_element_type=jnp.float32).reshape(shape4)
    k_raw = jnp.dot(tok_rows, w_key, preferred_element_type=jnp.float32).reshape(shape4)
    q_norm = scaled(q_raw, q_gain).astype(jnp.bfloat16)
    k_norm = scaled(k_raw, k_gain).astype(jnp.bfloat16)
    value = jnp.dot(tok_rows, w_value, preferred_element_type=jnp.float32).astype(jnp.bfloat16).reshape(shape4)
    cotan = grad_attn.reshape(shape4)
    d_qn, d_kn, d_val = attend_back(q_norm, k_norm, value, cotan)
    _, pull_query = jax.vjp(lambda raw: scaled(raw, q_gain), q_raw)
    _, pull_key = jax.vjp(lambda raw: scaled(raw, k_gain), k_raw)
    d_q_raw = pull_query(d_qn.astype(jnp.float32))[0].astype(jnp.bfloat16).reshape(FRAMES * PATCHES, D)
    d_k_raw = pull_key(d_kn.astype(jnp.float32))[0].astype(jnp.bfloat16).reshape(FRAMES * PATCHES, D)
    d_v_rows = d_val.reshape(FRAMES * PATCHES, D)
    contract = (((1,), (1,)), ((), ()))
    grad_sum = lax.dot_general(d_q_raw, w_query, contract, preferred_element_type=jnp.float32)
    grad_sum = grad_sum + lax.dot_general(d_k_raw, w_key, contract, preferred_element_type=jnp.float32)
    grad_sum = grad_sum + lax.dot_general(d_v_rows, w_value, contract, preferred_element_type=jnp.float32)
    grad_input = grad_sum.astype(jnp.bfloat16).reshape(FRAMES, PATCHES, D)
    d_all = jnp.concatenate([d_q_raw, d_k_raw, d_v_rows], axis=1)
    groups = tok_rows.reshape(N_FRAME, FR_DEV * PATCHES, D)
    d_groups = d_all.reshape(N_FRAME, FR_DEV * PATCHES, 3 * D)

    def add_group(total, pair):
        term = lax.dot_general(pair[0], pair[1], (((0,), (0,)), ((), ())), preferred_element_type=jnp.float32)
        rounded = lax.optimization_barrier(term.astype(jnp.bfloat16)).astype(jnp.float32)
        return (total + rounded, None)
    total, _ = lax.scan(add_group, jnp.zeros((D, 3 * D), jnp.float32), (groups, d_groups))
    return (grad_input, total[:, :D], total[:, D:2 * D], total[:, 2 * D:])
```

```python
import functools
import math

import jax
import jax.numpy as jnp
from jax import lax
from jax.experimental import pallas as pl
from jax.experimental.pallas import tpu as pltpu
from jax.sharding import Mesh, PartitionSpec as P

HD = 128
EPS = 1e-06
BF = jnp.bfloat16
F32 = jnp.float32


def send(array, axis, shift):
    n = lax.axis_size(axis)
    return lax.ppermute(array, axis, [(i, (i + shift) % n) for i in range(n)])


def ordered(mine, other, at, dim):
    first = jnp.where(at == 0, mine, other)
    second = jnp.where(at == 0, other, mine)
    return jnp.concatenate([first, second], axis=dim)


def spread(array, axis):
    half = array.shape[0] // 2
    one = send(array, axis, 1)
    three = send(array, axis, -1)
    two_a = send(one[:half], axis, 1)
    two_b = send(three[half:], axis, -1)
    return array, one, two_a, two_b, three


def added(a, b):
    return (a.astype(F32) + b.astype(F32)).astype(BF)


def gathered_sum(parts, axis):
    zero, one, two_a, two_b, three = parts
    half = two_a.shape[0]
    from_a = send(two_a, axis, -1)
    from_b = send(two_b, axis, 1)
    one = jnp.concatenate([added(one[:half], from_a), one[half:]], axis=0)
    three = jnp.concatenate([three[:half], added(three[half:], from_b)], axis=0)
    back = send(one, axis, -1)
    ahead = send(three, axis, 1)
    return zero.astype(F32) + back.astype(F32) + ahead.astype(F32)


def slot_of(block, y, c):
    return (((block & 1) ^ c) * 4 + (((block >> 1) - y) & 3)) * 2 + (block >> 3)


def pieces(w0, w1, w2a, w2b, w3):
    result = []
    for k, ref in ((0, w0), (1, w1), (3, w3)):
        for j in range(4):
            result.append((k, j, ref, j * 256))
    for j in range(4):
        result.append((2, j, w2a if j < 2 else w2b, (j % 2) * 256))
    return result


def main_kernel(
    place, act, w0, w1, w2a, w2b, w3, cot, qg, kg, d_out, g0, g1, g2, g3, raw, turned
):
    zh, x, y, c = place[0], place[1], place[2], place[3]

    def slot(k, j):
        return slot_of(((zh - j) & 3) * 4 + ((x - k) & 3), y, c)

    first = True
    for k, j, ref, row in pieces(w0, w1, w2a, w2b, w3):
        part = jnp.dot(act[slot(k, j)], ref[row : row + 256, :], preferred_element_type=F32)
        if first:
            raw[...] = part
            first = False
        else:
            raw[...] += part

    factor = 1.0 / math.sqrt(HD)
    q_gain = qg[...]
    k_gain = kg[...]
    nt = (((1,), (1,)), ((), ()))
    tn = (((0,), (0,)), ((), ()))
    dot = functools.partial(lax.dot_general, preferred_element_type=F32)
    plain = (((1,), (0,)), ((), ()))

    def back_norm(x_raw, inverse, gain, dy):
        gdy = gain * dy
        m = jnp.mean(x_raw * gdy, axis=-1, keepdims=True)
        return inverse * gdy - x_raw * (inverse * inverse * inverse * m)

    def patch(p, _):
        rows = pl.ds(pl.multiple_of(p * 64, 64), 64)
        q_raw = raw[rows, 0:128]
        k_raw = raw[rows, 128:256]
        value = raw[rows, 256:384].astype(BF)
        cotan = cot[rows, :]
        q_inv = lax.rsqrt(jnp.mean(q_raw * q_raw, axis=-1, keepdims=True) + EPS)
        k_inv = lax.rsqrt(jnp.mean(k_raw * k_raw, axis=-1, keepdims=True) + EPS)
        q_norm = (q_raw * q_inv * q_gain).astype(BF)
        k_norm = (k_raw * k_inv * k_gain).astype(BF)
        expon = jnp.exp(dot(q_norm, k_norm, nt) * factor)
        prob = expon / jnp.sum(expon, axis=-1, keepdims=True)
        d_prob = dot(cotan, value, nt)
        d_val = dot(prob.astype(BF), cotan, tn)
        d_score = prob * (d_prob - jnp.sum(prob * d_prob, axis=-1, keepdims=True)) * factor
        d_score = d_score.astype(BF)
        d_qn = dot(d_score, k_norm, plain).astype(BF).astype(F32)
        d_kn = dot(d_score, q_norm, tn).astype(BF).astype(F32)
        d_out[rows, 0:128] = back_norm(q_raw, q_inv, q_gain, d_qn).astype(BF)
        d_out[rows, 128:256] = back_norm(k_raw, k_inv, k_gain, d_kn).astype(BF)
        d_out[rows, 256:384] = d_val.astype(BF)
        return 0

    lax.fori_loop(0, act.shape[1] // 64, patch, 0, unroll=True)

    turned[...] = d_out[...].T
    outs = (g0, g1, g2, g3)
    for k in (2, 1, 3, 0):
        for j in range(4):
            outs[k][j] = jnp.dot(
                turned[...], act[slot(k, j)], preferred_element_type=F32
            ).astype(BF)


def input_kernel(place, da, db, *refs):
    zh, x, y, c = place[0], place[1], place[2], place[3]
    out = refs[10]
    nt = (((1,), (1,)), ((), ()))
    for (k, j, ref_a, row), (_, _, ref_b, _) in zip(pieces(*refs[:5]), pieces(*refs[5:10])):
        at = slot_of(((zh - j) & 3) * 4 + ((x - k) & 3), y, c)
        total = lax.dot_general(da[...], ref_a[row : row + 256, :], nt, preferred_element_type=F32)
        total += lax.dot_general(db[...], ref_b[row : row + 256, :], nt, preferred_element_type=F32)
        out[at] = total.astype(BF)


def vmem(count):
    return [pl.BlockSpec(memory_space=pltpu.VMEM)] * count


def main_call(place, act, weights, cot, q_gain, k_gain):
    tokens = act.shape[1]
    g = jax.ShapeDtypeStruct((4, 384, 256), BF)
    return pl.pallas_call(
        main_kernel,
        out_shape=[jax.ShapeDtypeStruct((tokens, 384), BF), g, g, g, g],
        in_specs=[pl.BlockSpec(memory_space=pltpu.SMEM)] + vmem(9),
        out_specs=vmem(5),
        scratch_shapes=[pltpu.VMEM((tokens, 384), F32), pltpu.VMEM((384, tokens), BF)],
        compiler_params=pltpu.CompilerParams(vmem_limit_bytes=40 * 2**20),
        cost_estimate=pl.CostEstimate(
            flops=4 * tokens * 4096 * 384, bytes_accessed=12 * 2**20, transcendentals=0
        ),
    )(place, act, *weights, cot, q_gain.reshape(1, HD), k_gain.reshape(1, HD))


def input_call(place, da, db, weights_a, weights_b):
    tokens = da.shape[0]
    return pl.pallas_call(
        input_kernel,
        out_shape=jax.ShapeDtypeStruct((16, tokens, 256), BF),
        in_specs=[pl.BlockSpec(memory_space=pltpu.SMEM)] + vmem(12),
        out_specs=pl.BlockSpec(memory_space=pltpu.VMEM),
        compiler_params=pltpu.CompilerParams(vmem_limit_bytes=40 * 2**20),
        cost_estimate=pl.CostEstimate(
            flops=4 * tokens * 4096 * 384, bytes_accessed=12 * 2**20, transcendentals=0
        ),
    )(place, da, db, *weights_a, *weights_b)


def body(activations, w_query, w_key, w_value, q_gain, k_gain, grad_attn):
    zh, x, c, zl, y = (lax.axis_index(a) for a in ("zh", "x", "c", "zl", "y"))
    place = jnp.stack([zh, x, y, c]).astype(jnp.int32)
    cut = lax.dynamic_slice_in_dim

    def columns(core, chunk):
        return jnp.concatenate(
            [cut(w, core * 256 + chunk * 128, 128, 1) for w in (w_query, w_key, w_value)], axis=1
        )

    weights = []
    for chunk in range(2):
        other = send(columns(1 - c, chunk), "c", 1)
        own = ordered(columns(c, chunk), other, c, 0)
        column = jnp.concatenate(spread(own, "zh"), axis=0)
        weights.append(spread(column, "x"))

    block = (zl * 4 + y) * 2

    def slices(core):
        return jnp.concatenate(
            [cut(activations, (block + core) * 256, 256, 2), cut(grad_attn, core * 256, 256, 2)],
            axis=2,
        )

    mixed = ordered(slices(c), send(slices(1 - c), "c", 1), c, 0)
    by_x = jnp.concatenate(
        [send(cut(mixed, ((x + d) & 3) * 32, 32, 1), "x", d) if d else cut(mixed, x * 32, 32, 1) for d in range(4)],
        axis=0,
    )
    by_z = jnp.concatenate(
        [send(cut(by_x, ((zh + d) & 3) * 8, 8, 1), "zh", d) if d else cut(by_x, zh * 8, 8, 1) for d in range(4)],
        axis=0,
    )
    tokens = by_z.transpose(1, 0, 2).reshape(512, 512)
    mine = tokens[:, :256]
    cot = tokens[:, 256:]
    pair = ordered(mine[None], send(mine, "zl", 1)[None], zl, 0)
    _, one, two_a, two_b, three = spread(pair, "y")
    along = jnp.concatenate([pair, three, two_a, two_b, one], axis=0)
    act = jnp.concatenate([along, send(along, "c", 1)], axis=0)

    sums = []
    grads = []
    for chunk in range(2):
        d_all, g0, g1, g2, g3 = main_call(
            place, act, weights[chunk], cot[:, chunk * 128 : chunk * 128 + 128], q_gain, k_gain
        )
        grads.append(d_all)
        over_x = gathered_sum((g0, g1, g2[:2], g2[2:], g3), "x").astype(BF)
        h2 = over_x[2]
        total = gathered_sum((over_x[0], over_x[1], h2[:192], h2[192:], over_x[3]), "zh")
        sums.append(total)

    part = input_call(place, grads[0], grads[1], weights[0], weights[1])
    part = added(part[:8], send(part[8:], "c", 1))
    part = part.reshape(4, 2, 512, 256)
    two = part[2]
    over_y = gathered_sum((part[0], part[3], two[:1], two[1:], part[1]), "y")
    ours = jnp.where(zl == 0, over_y[0], over_y[1])
    theirs = jnp.where(zl == 0, over_y[1], over_y[0]).astype(BF)
    result = (ours + send(theirs, "zl", 1).astype(F32)).astype(BF)

    result = result.reshape(8, 4, 16, 256)
    back_z = jnp.stack(
        [send(result[:, d], "zh", -d) if d else result[:, 0] for d in range(4)], axis=0
    )
    back_z = jnp.roll(back_z, zh, axis=0).reshape(32, 4, 4, 256)
    back_x = jnp.stack(
        [send(back_z[:, d], "x", -d) if d else back_z[:, 0] for d in range(4)], axis=0
    )
    back_x = jnp.roll(back_x, x, axis=0).reshape(128, 4, 256)
    keep = cut(back_x, c * 2, 2, 1)
    away = send(cut(back_x, (1 - c) * 2, 2, 1), "c", 1)
    grad_input = ordered(keep, away, c, 2).transpose(1, 0, 2)

    outs = [[], [], []]
    ready = []
    for total in sums:
        kept = cut(total, c * 128, 128, 1)
        other = send(cut(total, (1 - c) * 128, 128, 1).astype(BF), "c", 1).astype(F32)
        ready.append((jnp.where(c == 0, kept, other), jnp.where(c == 0, other, kept)))
    for core in range(2):
        for chunk in range(2):
            for which in range(3):
                outs[which].append(ready[chunk][core][which * 128 : which * 128 + 128].T)
    grad_wq, grad_wk, grad_wv = (jnp.concatenate(o, axis=1) for o in outs)
    return (grad_input, grad_wq, grad_wk, grad_wv)


def solution(mesh):
    fine = Mesh(mesh.devices.reshape(4, 4, 2, 2, 4), ("zh", "x", "c", "zl", "y"))
    frame = ("zh", "x", "c")
    head = ("zl", "y")
    weight = P(frame, head)
    return jax.shard_map(
        body,
        mesh=fine,
        in_specs=(P(frame, None, None), weight, weight, weight, P(), P(), P(frame, None, head)),
        out_specs=(P(frame, None, head), weight, weight, weight),
        check_vma=False,
    )
```

```python
import functools
import math

import jax
import jax.numpy as jnp
from jax import lax
from jax.experimental import pallas as pl
from jax.experimental.pallas import tpu as pltpu
from jax.sharding import Mesh, PartitionSpec as P

HD = 128
EPS = 1e-06
BF = jnp.bfloat16
F32 = jnp.float32
NT = (((1,), (1,)), ((), ()))
TN = (((0,), (0,)), ((), ()))
NN = (((1,), (0,)), ((), ()))
dot = functools.partial(lax.dot_general, preferred_element_type=F32)


def send(array, axis, shift):
    n = lax.axis_size(axis)
    return lax.ppermute(array, axis, [(i, (i + shift) % n) for i in range(n)])


def nothing(*refs):
    pass


def tie(arrays, after):
    where = pl.BlockSpec(memory_space=pl.ANY)
    return pl.pallas_call(
        nothing,
        out_shape=[jax.ShapeDtypeStruct(a.shape, a.dtype) for a in arrays],
        in_specs=[where] * (len(arrays) + len(after)),
        out_specs=[where] * len(arrays),
        input_output_aliases={i: i for i in range(len(arrays))},
        cost_estimate=pl.CostEstimate(flops=0, bytes_accessed=0, transcendentals=0),
    )(*arrays, *after)


def added(a, b):
    return (a.astype(F32) + b.astype(F32)).astype(BF)


def slot_of(half, block, y):
    return ((half * 4 + (((block >> 1) - y) & 3)) * 2 + (block >> 3)) * 2 + (block & 1)


def pieces(chunk, own, p1, p3, p2, a1, a3, a2, b1, b3, b2a, b2b):
    cut_at = 2 - chunk
    opposite = [b2a.at[i] for i in range(cut_at)] + [b2b.at[i] for i in range(3 - cut_at)]
    result = [(0, 0, own.at[chunk]), (1, 0, a1.at[chunk]), (3, 0, a3.at[chunk]), (2, 0, a2.at[0])]
    result += [(0, 1, p1.at[chunk]), (0, 3, p3.at[chunk]), (0, 2, p2.at[0])]
    for k, blocks in ((1, [b1.at[i] for i in range(3)]), (3, [b3.at[i] for i in range(3)]), (2, opposite)):
        result += [(k, j, ref) for j, ref in zip((1, 3, 2), blocks)]
    return result


WEIGHT_REFS = 11


def block_at(place, k, j):
    return ((place[0] - j) & 3) * 4 + ((place[1] - k) & 3)


def attention_kernel(chunk, place, act, cot, qg, kg, *refs):
    weights, (d_out, raw) = refs[:WEIGHT_REFS], refs[WEIGHT_REFS:]
    y = place[2]
    first = True
    for k, j, ref in pieces(chunk, *weights):
        block = block_at(place, k, j)
        for half in range(2):
            part = dot(act[slot_of(half, block, y)], ref[...], NN)
            rows = slice(half * 256, half * 256 + 256)
            if first:
                raw[rows, :] = part
            else:
                raw[rows, :] += part
        first = False

    factor = 1.0 / math.sqrt(HD)
    q_gain = qg[...]
    k_gain = kg[...]

    def back_norm(x_raw, inverse, gain, dy):
        gdy = gain * dy
        m = jnp.mean(x_raw * gdy, axis=-1, keepdims=True)
        return inverse * gdy - x_raw * (inverse * inverse * inverse * m)

    for p in range(8):
        a, b = slice(p * 32, p * 32 + 32), slice(256 + p * 32, 256 + p * 32 + 32)
        both = jnp.concatenate([raw[a, :], raw[b, :]], axis=0)
        q_raw, k_raw, value = both[:, 0:128], both[:, 128:256], both[:, 256:384].astype(BF)
        cols = slice(chunk * 128, chunk * 128 + 128)
        cotan = jnp.concatenate([cot[0, a, cols], cot[1, a, cols]], axis=0)
        q_inv = lax.rsqrt(jnp.mean(q_raw * q_raw, axis=-1, keepdims=True) + EPS)
        k_inv = lax.rsqrt(jnp.mean(k_raw * k_raw, axis=-1, keepdims=True) + EPS)
        q_norm = (q_raw * q_inv * q_gain).astype(BF)
        k_norm = (k_raw * k_inv * k_gain).astype(BF)
        expon = jnp.exp(dot(q_norm, k_norm, NT) * factor)
        prob = expon / jnp.sum(expon, axis=-1, keepdims=True)
        d_prob = dot(cotan, value, NT)
        d_val = dot(prob.astype(BF), cotan, TN)
        d_score = prob * (d_prob - jnp.sum(prob * d_prob, axis=-1, keepdims=True)) * factor
        d_score = d_score.astype(BF)
        d_qn = dot(d_score, k_norm, NN).astype(BF).astype(F32)
        d_kn = dot(d_score, q_norm, TN).astype(BF).astype(F32)
        d_q = back_norm(q_raw, q_inv, q_gain, d_qn).astype(BF)
        d_k = back_norm(k_raw, k_inv, k_gain, d_kn).astype(BF)
        for at, d in ((0, d_q), (128, d_k), (256, d_val.astype(BF))):
            d_out[a, at : at + 128] = d[:32]
            d_out[b, at : at + 128] = d[32:]


def term_kernel(place, act, d_all, g0, g1, g2, g3, turned):
    y = place[2]
    turned[...] = d_all[...].T
    outs = (g0, g1, g2, g3)
    for k in (2, 1, 3, 0):
        for j in range(4):
            block = block_at(place, k, j)
            total = dot(turned[:, 0:256], act[slot_of(0, block, y)], NN)
            total += dot(turned[:, 256:512], act[slot_of(1, block, y)], NN)
            outs[k][j] = total.astype(BF)


def input_kernel(place, da, db, *refs):
    y = place[2]
    out = refs[-1]
    of_a = pieces(0, *refs[:WEIGHT_REFS])
    of_b = pieces(1, *refs[WEIGHT_REFS : 2 * WEIGHT_REFS])
    for (k, j, ref_a), (_, _, ref_b) in zip(of_a, of_b):
        block = block_at(place, k, j)
        for half in range(2):
            rows = slice(half * 256, half * 256 + 256)
            total = dot(da[rows, :], ref_a[...], NT) + dot(db[rows, :], ref_b[...], NT)
            out[slot_of(half, block, y)] = total.astype(BF)


def call(kernel, out_shape, scratch, flops, place, *arrays):
    whole = pl.BlockSpec(memory_space=pltpu.VMEM)
    return pl.pallas_call(
        kernel,
        out_shape=out_shape,
        in_specs=[pl.BlockSpec(memory_space=pltpu.SMEM)] + [whole] * len(arrays),
        out_specs=jax.tree.map(lambda _: whole, out_shape),
        scratch_shapes=scratch,
        compiler_params=pltpu.CompilerParams(vmem_limit_bytes=40 * 2**20),
        cost_estimate=pl.CostEstimate(flops=flops, bytes_accessed=8 * 2**20, transcendentals=0),
    )(place, *arrays)


def body(activations, w_query, w_key, w_value, q_gain, k_gain, grad_attn):
    zh, x, c, zl, y = (lax.axis_index(a) for a in ("zh", "x", "c", "zl", "y"))
    place = jnp.stack([zh, x, y]).astype(jnp.int32)
    cut = lax.dynamic_slice_in_dim
    flops = 2 * 512 * 4096 * 384

    def columns(core):
        return jnp.stack(
            [
                jnp.concatenate(
                    [cut(w, core * 256 + q * 128, 128, 1) for w in (w_query, w_key, w_value)], axis=1
                )
                for q in range(2)
            ]
        )

    theirs = send(columns(1 - c), "c", 1)
    ours = columns(c)
    own = jnp.concatenate(
        [jnp.where(c == 0, ours, theirs), jnp.where(c == 0, theirs, ours)], axis=1
    )
    p1 = send(own, "zh", 1)
    p3 = send(own, "zh", -1)
    a1 = send(own, "x", 1)
    a3 = send(own, "x", -1)
    p2 = [send(p1[:1], "zh", 1), send(p3[1:], "zh", -1)]
    a2 = [send(a1[:1], "x", 1), send(a3[1:], "x", -1)]
    rest = [jnp.concatenate([p1[q : q + 1], p3[q : q + 1], p2[q]], axis=0) for q in range(2)]
    weights = []
    for q in range(2):
        source = rest[q]
        if q == 1:
            (source,) = tie([source], [b1, b3])
        b1 = send(source, "x", 1)
        b3 = send(source, "x", -1)
        at = 2 - q
        b2a = send(b1[:at], "x", 1)
        b2b = send(b3[at:], "x", -1)
        weights.append((own, p1, p3, p2[q], a1, a3, a2[q], b1, b3, b2a, b2b))

    head = zl * 4 + y
    mixed = jnp.concatenate([cut(activations, head * 512, 512, 2), grad_attn], axis=2)
    mixed = mixed.reshape(2, 16, 8, 1024).transpose(1, 2, 0, 3)
    mixed = lax.all_to_all(mixed, ("zh", "x"), 0, 0, tiled=True)
    tokens = mixed.transpose(1, 0, 2, 3).reshape(256, 1024)
    mine = jnp.stack([tokens[:, :256], tokens[:, 256:512]])
    cot_own = cut(tokens, 512 + c * 256, 256, 1)
    cot_other = send(cut(tokens, 512 + (1 - c) * 256, 256, 1), "c", 1)
    cot = jnp.stack([cot_own, cot_other])
    partner = send(mine, "zl", 1)
    pair = jnp.stack([jnp.where(zl == 0, mine, partner), jnp.where(zl == 0, partner, mine)])
    one = send(pair, "y", 1)
    three = send(pair, "y", -1)
    two_a = send(one[:1], "y", 1)
    two_b = send(three[1:], "y", -1)
    along = jnp.concatenate([pair, three, two_a, two_b, one], axis=0)
    act = jnp.stack([along, send(along, "c", 1)]).reshape(32, 256, 256)

    gains = (q_gain.reshape(1, HD), k_gain.reshape(1, HD))
    d_shape = jax.ShapeDtypeStruct((512, 384), BF)
    g_shape = [jax.ShapeDtypeStruct((4, 384, 256), BF)] * 4

    def attention(q):
        return call(
            functools.partial(attention_kernel, q),
            d_shape,
            [pltpu.VMEM((512, 384), F32)],
            flops,
            place,
            act,
            cot,
            *gains,
            *weights[q],
        )

    def terms(d_all):
        return call(term_kernel, g_shape, [pltpu.VMEM((384, 512), BF)], flops, place, act, d_all)

    def halves_x(g):
        return send(g[2][:2], "x", -1), send(g[2][2:], "x", 1)

    def whole_x(g, from_a, from_b):
        one = jnp.concatenate([added(g[1][:2], from_a), g[1][2:]], axis=0)
        three = jnp.concatenate([g[3][:2], added(g[3][2:], from_b)], axis=0)
        return send(one, "x", -1), send(three, "x", 1)

    def total_of(zero, back, ahead):
        return zero.astype(F32) + back.astype(F32) + ahead.astype(F32)

    def halves_z(s):
        return send(s[2][:192], "zh", -1), send(s[2][192:], "zh", 1)

    def whole_z(s, from_a, from_b):
        one = jnp.concatenate([added(s[1][:192], from_a), s[1][192:]], axis=0)
        three = jnp.concatenate([s[3][:192], added(s[3][192:], from_b)], axis=0)
        return send(one, "zh", -1), send(three, "zh", 1)

    d0 = attention(0)
    g_0 = terms(d0)
    half_0 = halves_x(g_0)
    d1 = attention(1)
    part = call(
        input_kernel,
        jax.ShapeDtypeStruct((32, 256, 256), BF),
        [],
        2 * flops,
        place,
        d0,
        d1,
        *weights[0],
        *weights[1],
    )
    (d1,) = tie([d1], [part])
    got = send(part[16:], "c", 1)
    (part, got) = (part[:16], got)
    whole_0 = whole_x(g_0, *half_0)
    g_1 = list(terms(d1))
    (g_1[2],) = tie([g_1[2]], [got])
    half_1 = halves_x(g_1)

    part = added(part, got).reshape(4, 2, 2, 256, 256)
    y_a, y_b = send(part[2][:1], "y", -1), send(part[2][1:], "y", 1)
    y_one = jnp.concatenate([added(part[3][:1], y_a), part[3][1:]], axis=0)
    y_three = jnp.concatenate([part[1][:1], added(part[1][1:], y_b)], axis=0)
    back, ahead = send(y_one, "y", -1), send(y_three, "y", 1)

    s_0 = total_of(g_0[0], *whole_0).astype(BF)
    whole_1 = whole_x(g_1, *half_1)
    (s_0,) = tie([s_0], [y_a, y_b])
    z_half_0 = halves_z(s_0)
    over_y = total_of(part[0], back, ahead)
    keep = jnp.where(zl == 0, over_y[0], over_y[1])
    away = jnp.where(zl == 0, over_y[1], over_y[0]).astype(BF)
    partner = send(away, "zl", 1)
    z_whole_0 = whole_z(s_0, *z_half_0)

    s_1 = total_of(g_1[0], *whole_1).astype(BF)
    (s_1,) = tie([s_1], [partner])
    z_half_1 = halves_z(s_1)
    z_whole_1 = whole_z(s_1, *z_half_1)

    result = (keep + partner.astype(F32)).astype(BF)
    result = result.reshape(2, 8, 16, 2, 256).transpose(2, 1, 3, 0, 4).reshape(16, 8, 2, 512)
    result = lax.all_to_all(result, ("zh", "x"), 0, 0, tiled=True)
    grad_input = result.reshape(128, 2, 512).transpose(1, 0, 2)

    both = jnp.stack([total_of(s_0[0], *z_whole_0), total_of(s_1[0], *z_whole_1)])
    kept = cut(both, c * 128, 128, 2)
    other = send(cut(both, (1 - c) * 128, 128, 2).astype(BF), "c", 1).astype(F32)
    heads = jnp.concatenate([jnp.where(c == 0, kept, other), jnp.where(c == 0, other, kept)], axis=0)
    heads = heads.reshape(4, 3, 128, 128).transpose(1, 3, 0, 2).reshape(3, 128, 512)
    return (grad_input, heads[0], heads[1], heads[2])


def solution(mesh):
    fine = Mesh(mesh.devices.reshape(4, 4, 2, 2, 4), ("zh", "x", "c", "zl", "y"))
    frame = ("zh", "x", "c")
    head = ("zl", "y")
    weight = P(frame, head)
    return jax.shard_map(
        body,
        mesh=fine,
        in_specs=(P(frame, None, None), weight, weight, weight, P(), P(), P(frame, None, head)),
        out_specs=(P(frame, None, head), weight, weight, weight),
        check_vma=False,
    )
```

```python
import functools
import math

import jax
import jax.numpy as jnp
from jax import lax
from jax.experimental import pallas as pl
from jax.experimental.pallas import tpu as pltpu
from jax.sharding import Mesh, PartitionSpec as P

HD = 128
EPS = 1e-06
BF = jnp.bfloat16
F32 = jnp.float32
NT = (((1,), (1,)), ((), ()))
TN = (((0,), (0,)), ((), ()))
NN = (((1,), (0,)), ((), ()))
dot = functools.partial(lax.dot_general, preferred_element_type=F32)


def send(array, axis, shift):
    n = lax.axis_size(axis)
    return lax.ppermute(array, axis, [(i, (i + shift) % n) for i in range(n)])


def nothing(*refs):
    pass


def tie(arrays, after):
    where = pl.BlockSpec(memory_space=pl.ANY)
    return pl.pallas_call(
        nothing,
        out_shape=[jax.ShapeDtypeStruct(a.shape, a.dtype) for a in arrays],
        in_specs=[where] * (len(arrays) + len(after)),
        out_specs=[where] * len(arrays),
        input_output_aliases={i: i for i in range(len(arrays))},
        cost_estimate=pl.CostEstimate(flops=0, bytes_accessed=0, transcendentals=0),
    )(*arrays, *after)


def added(a, b):
    return (a.astype(F32) + b.astype(F32)).astype(BF)


def slot_of(block, y):
    return ((((block >> 1) - y) & 3) * 2 + (block >> 3)) * 2 + (block & 1)


def pieces(chunk, own, p1, p3, p2, a1, a3, a2, b1, b3, b2a, b2b):
    cut_at = 2 - chunk
    opposite = [b2a.at[i] for i in range(cut_at)] + [b2b.at[i] for i in range(3 - cut_at)]
    result = [(0, 0, own.at[chunk]), (1, 0, a1.at[chunk]), (3, 0, a3.at[chunk]), (2, 0, a2.at[0])]
    result += [(0, 1, p1.at[chunk]), (0, 3, p3.at[chunk]), (0, 2, p2.at[0])]
    for k, blocks in ((1, [b1.at[i] for i in range(3)]), (3, [b3.at[i] for i in range(3)]), (2, opposite)):
        result += [(k, j, ref) for j, ref in zip((1, 3, 2), blocks)]
    return result


WEIGHT_REFS = 11


def block_at(place, k, j):
    return ((place[0] - j) & 3) * 4 + ((place[1] - k) & 3)


def attention_kernel(chunk, place, act, act_other, cot, qg, kg, *refs):
    weights, (d_out, raw) = refs[:WEIGHT_REFS], refs[WEIGHT_REFS:]
    y = place[2]
    first = True
    for k, j, ref in pieces(chunk, *weights):
        block = block_at(place, k, j)
        for half, held in enumerate((act, act_other)):
            part = dot(held[slot_of(block, y)], ref[...], NN)
            rows = slice(half * 256, half * 256 + 256)
            if first:
                raw[rows, :] = part
            else:
                raw[rows, :] += part
        first = False

    factor = 1.0 / math.sqrt(HD)
    q_gain = qg[0:1, :]
    k_gain = kg[0:1, :]

    def back_norm(x_raw, inverse, gain, dy):
        gdy = gain * dy
        m = jnp.mean(x_raw * gdy, axis=-1, keepdims=True)
        return inverse * gdy - x_raw * (inverse * inverse * inverse * m)

    for p in range(8):
        a, b = slice(p * 32, p * 32 + 32), slice(256 + p * 32, 256 + p * 32 + 32)
        both = jnp.concatenate([raw[a, :], raw[b, :]], axis=0)
        q_raw, k_raw, value = both[:, 0:128], both[:, 128:256], both[:, 256:384].astype(BF)
        cols = slice(chunk * 128, chunk * 128 + 128)
        cotan = jnp.concatenate([cot[0, a, cols], cot[1, a, cols]], axis=0)
        q_inv = lax.rsqrt(jnp.mean(q_raw * q_raw, axis=-1, keepdims=True) + EPS)
        k_inv = lax.rsqrt(jnp.mean(k_raw * k_raw, axis=-1, keepdims=True) + EPS)
        q_norm = (q_raw * q_inv * q_gain).astype(BF)
        k_norm = (k_raw * k_inv * k_gain).astype(BF)
        expon = jnp.exp(dot(q_norm, k_norm, NT) * factor)
        prob = expon / jnp.sum(expon, axis=-1, keepdims=True)
        d_prob = dot(cotan, value, NT)
        d_val = dot(prob.astype(BF), cotan, TN)
        d_score = prob * (d_prob - jnp.sum(prob * d_prob, axis=-1, keepdims=True)) * factor
        d_score = d_score.astype(BF)
        d_qn = dot(d_score, k_norm, NN).astype(BF).astype(F32)
        d_kn = dot(d_score, q_norm, TN).astype(BF).astype(F32)
        d_q = back_norm(q_raw, q_inv, q_gain, d_qn).astype(BF)
        d_k = back_norm(k_raw, k_inv, k_gain, d_kn).astype(BF)
        for at, d in ((0, d_q), (128, d_k), (256, d_val.astype(BF))):
            d_out[a, at : at + 128] = d[:32]
            d_out[b, at : at + 128] = d[32:]


def term_kernel(place, act, act_other, d_all, back, ahead, back_late, ahead_late, here, turned):
    y = place[2]
    turned[...] = d_all[...].T
    plan = [(back, i, k, j) for i, (k, j) in enumerate(((2, 0), (2, 1), (1, 2), (1, 3)))]
    plan += [(ahead, i, k, j) for i, (k, j) in enumerate(((2, 2), (2, 3), (3, 0), (3, 1)))]
    plan += [(back_late, j, 1, j) for j in range(2)]
    plan += [(ahead_late, j, 3, j + 2) for j in range(2)]
    plan += [(here, j, 0, j) for j in range(4)]
    for ref, i, k, j in plan:
        slot = slot_of(block_at(place, k, j), y)
        total = dot(turned[:, 0:256], act[slot], NN) + dot(turned[:, 256:512], act_other[slot], NN)
        ref[i] = total.astype(BF)


def input_kernel(place, da, db, *refs):
    y = place[2]
    outs = refs[-2:]
    of_a = pieces(0, *refs[:WEIGHT_REFS])
    of_b = pieces(1, *refs[WEIGHT_REFS : 2 * WEIGHT_REFS])
    for (k, j, ref_a), (_, _, ref_b) in zip(of_a, of_b):
        block = block_at(place, k, j)
        for half in range(2):
            rows = slice(half * 256, half * 256 + 256)
            total = dot(da[rows, :], ref_a[...], NT) + dot(db[rows, :], ref_b[...], NT)
            outs[half][slot_of(block, y)] = total.astype(BF)


def call(kernel, out_shape, scratch, flops, place, *arrays):
    whole = pl.BlockSpec(memory_space=pltpu.VMEM)
    return pl.pallas_call(
        kernel,
        out_shape=out_shape,
        in_specs=[pl.BlockSpec(memory_space=pltpu.SMEM)] + [whole] * len(arrays),
        out_specs=jax.tree.map(lambda _: whole, out_shape),
        scratch_shapes=scratch,
        compiler_params=pltpu.CompilerParams(vmem_limit_bytes=40 * 2**20),
        cost_estimate=pl.CostEstimate(flops=flops, bytes_accessed=8 * 2**20, transcendentals=0),
    )(place, *arrays)


def body(activations, w_query, w_key, w_value, q_gain, k_gain, grad_attn):
    zh, x, c, zl, y = (lax.axis_index(a) for a in ("zh", "x", "c", "zl", "y"))
    place = jnp.stack([zh, x, y]).astype(jnp.int32)
    cut = lax.dynamic_slice_in_dim
    flops = 2 * 512 * 4096 * 384

    def columns(core):
        return jnp.stack(
            [
                jnp.concatenate(
                    [cut(w, core * 256 + q * 128, 128, 1) for w in (w_query, w_key, w_value)], axis=1
                )
                for q in range(2)
            ]
        )

    theirs = send(columns(1 - c), "c", 1)
    ours = columns(c)
    own = jnp.concatenate(
        [jnp.where(c == 0, ours, theirs), jnp.where(c == 0, theirs, ours)], axis=1
    )
    p1 = send(own, "zh", 1)
    p3 = send(own, "zh", -1)
    a1 = send(own, "x", 1)
    a3 = send(own, "x", -1)

    head = zl * 4 + y
    mixed = jnp.concatenate([cut(activations, head * 512, 512, 2), grad_attn], axis=2)
    mixed = mixed.reshape(2, 16, 8, 1024).transpose(1, 2, 0, 3)

    on = tie([p1[:1], p3[1:], a1[:1], a3[1:], mixed], [p1, p3, a1, a3])
    p2 = [send(on[0], "zh", 1), send(on[1], "zh", -1)]
    a2 = [send(on[2], "x", 1), send(on[3], "x", -1)]
    mixed = lax.all_to_all(on[4], ("zh", "x"), 0, 0, tiled=True)
    tokens = mixed.transpose(1, 0, 2, 3).reshape(256, 1024)
    mine = jnp.stack([tokens[:, :256], tokens[:, 256:512]])
    cot_own = cut(tokens, 512 + c * 256, 256, 1)
    cot_other = send(cut(tokens, 512 + (1 - c) * 256, 256, 1), "c", 1)
    cot = jnp.stack([cot_own, cot_other])

    rest = [jnp.concatenate([p1[q : q + 1], p3[q : q + 1], p2[q]], axis=0) for q in range(2)]

    on = tie([rest[0], mine], [*p2, *a2])
    rest[0], mine = on
    b1, b3 = [send(rest[0], "x", 1)], [send(rest[0], "x", -1)]
    partner = send(mine, "zl", 1)
    pair = jnp.stack([jnp.where(zl == 0, mine, partner), jnp.where(zl == 0, partner, mine)])

    on = tie([b1[0][:2], b3[0][2:], pair], [b1[0], b3[0]])
    pair = on[2]
    b2a, b2b = [send(on[0], "x", 1)], [send(on[1], "x", -1)]
    one = send(pair, "y", 1)
    three = send(pair, "y", -1)

    on = tie([rest[1], one[:1], three[1:]], [b2a[0], b2b[0], one, three])
    b1.append(send(on[0], "x", 1))
    b3.append(send(on[0], "x", -1))
    two_a = send(on[1], "y", 1)
    two_b = send(on[2], "y", -1)
    act = jnp.concatenate([pair, three, two_a, two_b, one], axis=0).reshape(16, 256, 256)

    on = tie([b1[1][:1], b3[1][1:], act], [b1[1], b3[1]])
    b2a.append(send(on[0], "x", 1))
    b2b.append(send(on[1], "x", -1))
    act = on[2]
    act_other = send(act, "c", 1)
    weights = [
        (own, p1, p3, p2[q], a1, a3, a2[q], b1[q], b3[q], b2a[q], b2b[q]) for q in range(2)
    ]

    d_shape = jax.ShapeDtypeStruct((512, 384), BF)
    g_shape = [jax.ShapeDtypeStruct((n, 384, 256), BF) for n in (4, 4, 2, 2, 4)]
    part_shape = [jax.ShapeDtypeStruct((16, 256, 256), BF)] * 2
    gains = [jnp.stack([q_gain, q_gain]), jnp.stack([k_gain, k_gain])]

    def attention(q, gains):
        scratch = [pltpu.VMEM((512, 384), F32)]
        kernel = functools.partial(attention_kernel, q)
        return call(kernel, d_shape, scratch, flops, place, act, act_other, cot, *gains, *weights[q])

    def terms(d_all):
        scratch = [pltpu.VMEM((384, 512), BF)]
        return call(term_kernel, g_shape, scratch, flops, place, act, act_other, d_all)

    def total_of(zero, back, ahead):
        return zero.astype(F32) + back.astype(F32) + ahead.astype(F32)

    def late(g, first, axis):
        n = g[2].shape[0]
        back = send(added(g[2], first[0][:n]), axis, -1)
        ahead = send(added(g[3], first[1][:n]), axis, 1)
        return back, ahead

    def finish(g, first, second):
        n = g[2].shape[0]
        from_ahead = jnp.concatenate([second[0], first[0][n:]], axis=0)
        from_behind = jnp.concatenate([first[1][n:], second[1]], axis=0)
        return total_of(g[4], from_ahead, from_behind)

    def early(g, axis):
        return send(g[0], axis, -1), send(g[1], axis, 1)

    def split_z(s):
        half = s.shape[1] // 2
        back = jnp.concatenate([s[2, :half], s[1, half:]], axis=0)
        ahead = jnp.concatenate([s[2, half:], s[3, :half]], axis=0)
        return [back, ahead, s[1, :half], s[3, half:], s[0]]

    d0 = attention(0, gains)
    g_0 = terms(d0)
    x_early_0 = early(g_0, "x")
    d1 = attention(1, tie(gains, [g_0[0]]))
    part, theirs = call(
        input_kernel, part_shape, [], 2 * flops, place, d0, d1, *weights[0], *weights[1]
    )
    (d1,) = tie([d1], [part])
    got = send(theirs, "c", 1)
    g_1 = list(terms(d1))
    x_late_0 = late(g_0, x_early_0, "x")

    part = added(part, got).reshape(4, 2, 2, 256, 256)
    y_back = jnp.concatenate([part[2][:1], part[3][1:]], axis=0)
    y_ahead = jnp.concatenate([part[2][1:], part[1][:1]], axis=0)
    g_y = [y_back, y_ahead, part[3][:1], part[1][1:], part[0]]
    y_early = early(g_y, "y")
    y_late = late(g_y, y_early, "y")

    g_1[0], g_1[1] = tie(g_1[:2], [got, x_early_0[0], x_early_0[1]])
    x_early_1 = early(g_1, "x")
    s_0 = split_z(finish(g_0, x_early_0, x_late_0).astype(BF))
    s_0[0], s_0[1] = tie(s_0[:2], list(y_early))
    z_early_0 = early(s_0, "zh")
    x_late_1 = late(g_1, x_early_1, "x")

    over_y = finish(g_y, y_early, y_late)
    keep = jnp.where(zl == 0, over_y[0], over_y[1])
    away = jnp.where(zl == 0, over_y[1], over_y[0]).astype(BF)
    partner = send(away, "zl", 1)
    z_late_0 = late(s_0, z_early_0, "zh")

    result = (keep + partner.astype(F32)).astype(BF)
    result = result.reshape(2, 8, 16, 2, 256).transpose(2, 1, 3, 0, 4).reshape(16, 8, 2, 512)
    result = lax.all_to_all(result, ("zh", "x"), 0, 0, tiled=True)
    grad_input = result.reshape(128, 2, 512).transpose(1, 0, 2)

    s_1 = split_z(finish(g_1, x_early_1, x_late_1).astype(BF))
    s_1[0], s_1[1] = tie(s_1[:2], [partner])
    z_early_1 = early(s_1, "zh")
    late_operands = [added(s_1[2], z_early_1[0][:192]), added(s_1[3], z_early_1[1][:192])]
    late_operands = tie(late_operands, [result])
    z_late_1 = (send(late_operands[0], "zh", -1), send(late_operands[1], "zh", 1))

    both = jnp.stack([finish(s_0, z_early_0, z_late_0), finish(s_1, z_early_1, z_late_1)])
    kept = cut(both, c * 128, 128, 2)
    other = send(cut(both, (1 - c) * 128, 128, 2).astype(BF), "c", 1).astype(F32)
    heads = jnp.concatenate([jnp.where(c == 0, kept, other), jnp.where(c == 0, other, kept)], axis=0)
    heads = heads.reshape(4, 3, 128, 128).transpose(1, 3, 0, 2).reshape(3, 128, 512)
    return (grad_input, heads[0], heads[1], heads[2])


def solution(mesh):
    fine = Mesh(mesh.devices.reshape(4, 4, 2, 2, 4), ("zh", "x", "c", "zl", "y"))
    frame = ("zh", "x", "c")
    head = ("zl", "y")
    weight = P(frame, head)
    return jax.shard_map(
        body,
        mesh=fine,
        in_specs=(P(frame, None, None), weight, weight, weight, P(), P(), P(frame, None, head)),
        out_specs=(P(frame, None, head), weight, weight, weight),
        check_vma=False,
    )
```

```python
import functools
import math

import jax
import jax.numpy as jnp
from jax import lax
from jax.experimental import pallas as pl
from jax.experimental.pallas import tpu as pltpu
from jax.sharding import Mesh, PartitionSpec as P

HD = 128
EPS = 1e-06
BF = jnp.bfloat16
F32 = jnp.float32
NT = (((1,), (1,)), ((), ()))
TN = (((0,), (0,)), ((), ()))
NN = (((1,), (0,)), ((), ()))
dot = functools.partial(lax.dot_general, preferred_element_type=F32)


def send(array, axis, shift):
    n = lax.axis_size(axis)
    return lax.ppermute(array, axis, [(i, (i + shift) % n) for i in range(n)])


def nothing(*refs):
    pass


def tie(arrays, after):
    where = pl.BlockSpec(memory_space=pl.ANY)
    return pl.pallas_call(
        nothing,
        out_shape=[jax.ShapeDtypeStruct(a.shape, a.dtype) for a in arrays],
        in_specs=[where] * (len(arrays) + len(after)),
        out_specs=[where] * len(arrays),
        input_output_aliases={i: i for i in range(len(arrays))},
        cost_estimate=pl.CostEstimate(flops=0, bytes_accessed=0, transcendentals=0),
    )(*arrays, *after)


def added(a, b):
    return (a.astype(F32) + b.astype(F32)).astype(BF)


def slot_of(block, y):
    return ((((block >> 1) - y) & 3) * 2 + (block >> 3)) * 2 + (block & 1)


def block_at(place, k, j):
    return ((place[0] - j) & 3) * 4 + ((place[1] - k) & 3)


def attention_kernel(chunk, place, act, act_other, cot, qg, kg, weights, d_out, raw):
    y = place[2]
    for block in range(16):
        for half, held in enumerate((act, act_other)):
            part = dot(held[slot_of(block, y)], weights[block, chunk], NN)
            rows = slice(half * 256, half * 256 + 256)
            if block == 0:
                raw[rows, :] = part
            else:
                raw[rows, :] += part

    factor = 1.0 / math.sqrt(HD)
    q_gain = qg[0:1, :]
    k_gain = kg[0:1, :]

    def back_norm(x_raw, inverse, gain, dy):
        gdy = gain * dy
        m = jnp.mean(x_raw * gdy, axis=-1, keepdims=True)
        return inverse * gdy - x_raw * (inverse * inverse * inverse * m)

    for p in range(8):
        a, b = slice(p * 32, p * 32 + 32), slice(256 + p * 32, 256 + p * 32 + 32)
        both = jnp.concatenate([raw[a, :], raw[b, :]], axis=0)
        q_raw, k_raw, value = both[:, 0:128], both[:, 128:256], both[:, 256:384].astype(BF)
        cols = slice(chunk * 128, chunk * 128 + 128)
        cotan = jnp.concatenate([cot[0, a, cols], cot[1, a, cols]], axis=0)
        q_inv = lax.rsqrt(jnp.mean(q_raw * q_raw, axis=-1, keepdims=True) + EPS)
        k_inv = lax.rsqrt(jnp.mean(k_raw * k_raw, axis=-1, keepdims=True) + EPS)
        q_norm = (q_raw * q_inv * q_gain).astype(BF)
        k_norm = (k_raw * k_inv * k_gain).astype(BF)
        expon = jnp.exp(dot(q_norm, k_norm, NT) * factor)
        prob = expon / jnp.sum(expon, axis=-1, keepdims=True)
        d_prob = dot(cotan, value, NT)
        d_val = dot(prob.astype(BF), cotan, TN)
        d_score = prob * (d_prob - jnp.sum(prob * d_prob, axis=-1, keepdims=True)) * factor
        d_score = d_score.astype(BF)
        d_qn = dot(d_score, k_norm, NN).astype(BF).astype(F32)
        d_kn = dot(d_score, q_norm, TN).astype(BF).astype(F32)
        d_q = back_norm(q_raw, q_inv, q_gain, d_qn).astype(BF)
        d_k = back_norm(k_raw, k_inv, k_gain, d_kn).astype(BF)
        for at, d in ((0, d_q), (128, d_k), (256, d_val.astype(BF))):
            d_out[a, at : at + 128] = d[:32]
            d_out[b, at : at + 128] = d[32:]


def term_kernel(place, act, act_other, d_all, back, ahead, back_late, ahead_late, here, mark, turned):
    y = place[2]
    mark[...] = jnp.zeros_like(mark)
    turned[...] = d_all[...].T
    plan = [(back, i, k, j) for i, (k, j) in enumerate(((2, 0), (2, 1), (1, 2), (1, 3)))]
    plan += [(ahead, i, k, j) for i, (k, j) in enumerate(((2, 2), (2, 3), (3, 0), (3, 1)))]
    plan += [(back_late, j, 1, j) for j in range(2)]
    plan += [(ahead_late, j, 3, j + 2) for j in range(2)]
    plan += [(here, j, 0, j) for j in range(4)]
    for ref, i, k, j in plan:
        slot = slot_of(block_at(place, k, j), y)
        total = dot(turned[:, 0:256], act[slot], NN) + dot(turned[:, 256:512], act_other[slot], NN)
        ref[i] = total.astype(BF)


def input_kernel(place, da, db, weights, near, far):
    for block in range(16):
        for half, out in enumerate((near, far)):
            rows = slice(half * 256, half * 256 + 256)
            total = dot(da[rows, :], weights[block, 0], NT)
            total += dot(db[rows, :], weights[block, 1], NT)
            out[block] = total.astype(BF)


def call(kernel, out_shape, scratch, place, *arrays):
    whole = pl.BlockSpec(memory_space=pltpu.VMEM)
    return pl.pallas_call(
        kernel,
        out_shape=out_shape,
        in_specs=[pl.BlockSpec(memory_space=pltpu.SMEM)] + [whole] * len(arrays),
        out_specs=jax.tree.map(lambda _: whole, out_shape),
        scratch_shapes=scratch,
        compiler_params=pltpu.CompilerParams(vmem_limit_bytes=16 * 2**20),
        cost_estimate=pl.CostEstimate(flops=2**20, bytes_accessed=2**10, transcendentals=0),
    )(place, *arrays)


def body(activations, w_query, w_key, w_value, q_gain, k_gain, grad_attn):
    zh, x, c, zl, y = (lax.axis_index(a) for a in ("zh", "x", "c", "zl", "y"))
    place = jnp.stack([zh, x, y]).astype(jnp.int32)
    cut = lax.dynamic_slice_in_dim

    def columns(core):
        return jnp.stack(
            [
                jnp.concatenate(
                    [cut(w, core * 256 + q * 128, 128, 1) for w in (w_query, w_key, w_value)], axis=1
                )
                for q in range(2)
            ]
        )

    theirs = send(columns(1 - c), "c", 1)
    ours = columns(c)
    own = jnp.concatenate(
        [jnp.where(c == 0, ours, theirs), jnp.where(c == 0, theirs, ours)], axis=1
    )
    weights = lax.all_gather(own, ("zh", "x"), axis=0)

    head = zl * 4 + y
    mixed = jnp.concatenate([cut(activations, head * 512, 512, 2), grad_attn], axis=2)
    mixed = mixed.reshape(2, 16, 8, 1024).transpose(1, 2, 0, 3)

    (mixed,) = tie([mixed], [theirs])
    mixed = lax.all_to_all(mixed, ("zh", "x"), 0, 0, tiled=True)
    tokens = mixed.transpose(1, 0, 2, 3).reshape(256, 1024)
    mine = jnp.stack([tokens[:, :256], tokens[:, 256:512]])
    cot_own = cut(tokens, 512 + c * 256, 256, 1)
    cot_other = send(cut(tokens, 512 + (1 - c) * 256, 256, 1), "c", 1)
    cot = jnp.stack([cot_own, cot_other])
    partner = send(mine, "zl", 1)
    pair = jnp.stack([jnp.where(zl == 0, mine, partner), jnp.where(zl == 0, partner, mine)])
    one = send(pair, "y", 1)
    three = send(pair, "y", -1)
    two_a = send(one[:1], "y", 1)
    two_b = send(three[1:], "y", -1)
    act = jnp.concatenate([pair, three, two_a, two_b, one], axis=0).reshape(16, 256, 256)
    act_other = send(act, "c", 1)

    d_shape = jax.ShapeDtypeStruct((512, 384), BF)
    g_shape = [jax.ShapeDtypeStruct((n, 384, 256), BF) for n in (4, 4, 2, 2, 4)]
    g_shape.append(jax.ShapeDtypeStruct((8, 128), F32))
    part_shape = [jax.ShapeDtypeStruct((16, 256, 256), BF)] * 2
    gains = [jnp.stack([q_gain, q_gain]), jnp.stack([k_gain, k_gain])]

    def attention(q, gains):
        scratch = [pltpu.VMEM((512, 384), F32)]
        kernel = functools.partial(attention_kernel, q)
        return call(kernel, d_shape, scratch, place, act, act_other, cot, *gains, weights)

    def terms(d_all):
        scratch = [pltpu.VMEM((384, 512), BF)]
        return call(term_kernel, g_shape, scratch, place, act, act_other, d_all)

    def total_of(zero, back, ahead):
        return zero.astype(F32) + back.astype(F32) + ahead.astype(F32)

    def late(g, first, axis):
        n = g[2].shape[0]
        back = send(added(g[2], first[0][:n]), axis, -1)
        ahead = send(added(g[3], first[1][:n]), axis, 1)
        return back, ahead

    def finish(g, first, second):
        n = g[2].shape[0]
        from_ahead = jnp.concatenate([second[0], first[0][n:]], axis=0)
        from_behind = jnp.concatenate([first[1][n:], second[1]], axis=0)
        return total_of(g[4], from_ahead, from_behind)

    def early(g, axis):
        return send(g[0], axis, -1), send(g[1], axis, 1)

    def split_z(s):
        half = s.shape[1] // 2
        back = jnp.concatenate([s[2, :half], s[1, half:]], axis=0)
        ahead = jnp.concatenate([s[2, half:], s[3, :half]], axis=0)
        return [back, ahead, s[1, :half], s[3, half:], s[0]]

    d0 = attention(0, gains)
    g_0 = terms(d0)
    x_early_0 = early(g_0, "x")
    d1 = attention(1, tie(gains, [g_0[5]]))
    part, far = call(input_kernel, part_shape, [], place, d0, d1, weights)
    d1, far = tie([d1, far], [a[0, :16, :128] for a in x_early_0])
    got = send(far, "c", 1)
    g_1 = terms(d1)
    x_late_0 = late(g_0, x_early_0, "x")
    x_early_1 = early(g_1, "x")

    part = added(part, got)
    result = lax.psum_scatter(part, ("zl", "y"), scatter_dimension=0, tiled=True)

    s_0 = split_z(finish(g_0, x_early_0, x_late_0).astype(BF))
    z_early_0 = early(s_0, "zh")
    x_late_1 = late(g_1, x_early_1, "x")

    z_late_0 = late(s_0, z_early_0, "zh")

    result = result.reshape(2, 8, 16, 2, 256).transpose(2, 1, 3, 0, 4).reshape(16, 8, 2, 512)
    result = lax.all_to_all(result, ("zh", "x"), 0, 0, tiled=True)
    grad_input = result.reshape(128, 2, 512).transpose(1, 0, 2)

    s_1 = split_z(finish(g_1, x_early_1, x_late_1).astype(BF))
    z_early_1 = early(s_1, "zh")
    late_operands = [added(s_1[2], z_early_1[0][:192]), added(s_1[3], z_early_1[1][:192])]
    late_operands = tie(late_operands, [result])
    z_late_1 = (send(late_operands[0], "zh", -1), send(late_operands[1], "zh", 1))

    both = jnp.stack([finish(s_0, z_early_0, z_late_0), finish(s_1, z_early_1, z_late_1)])
    kept = cut(both, c * 128, 128, 2)
    other = send(cut(both, (1 - c) * 128, 128, 2).astype(BF), "c", 1).astype(F32)
    heads = jnp.concatenate([jnp.where(c == 0, kept, other), jnp.where(c == 0, other, kept)], axis=0)
    heads = heads.reshape(4, 3, 128, 128).transpose(1, 3, 0, 2).reshape(3, 128, 512)
    return (grad_input, heads[0], heads[1], heads[2])


def solution(mesh):
    fine = Mesh(mesh.devices.reshape(4, 4, 2, 2, 4), ("zh", "x", "c", "zl", "y"))
    frame = ("zh", "x", "c")
    head = ("zl", "y")
    weight = P(frame, head)
    return jax.shard_map(
        body,
        mesh=fine,
        in_specs=(P(frame, None, None), weight, weight, weight, P(), P(), P(frame, None, head)),
        out_specs=(P(frame, None, head), weight, weight, weight),
        check_vma=False,
    )
```

```python
import functools
import math

import jax
import jax.numpy as jnp
from jax import lax
from jax.experimental import pallas as pl
from jax.experimental.pallas import tpu as pltpu
from jax.sharding import Mesh, PartitionSpec as P

HD = 128
EPS = 1e-06
BF = jnp.bfloat16
F32 = jnp.float32
NT = (((1,), (1,)), ((), ()))
TN = (((0,), (0,)), ((), ()))
NN = (((1,), (0,)), ((), ()))
dot = functools.partial(lax.dot_general, preferred_element_type=F32)


def send(array, axis, shift):
    n = lax.axis_size(axis)
    return lax.ppermute(array, axis, [(i, (i + shift) % n) for i in range(n)])


def nothing(*refs):
    pass


def tie(arrays, after):
    where = pl.BlockSpec(memory_space=pl.ANY)
    return pl.pallas_call(
        nothing,
        out_shape=[jax.ShapeDtypeStruct(a.shape, a.dtype) for a in arrays],
        in_specs=[where] * (len(arrays) + len(after)),
        out_specs=[where] * len(arrays),
        input_output_aliases={i: i for i in range(len(arrays))},
        cost_estimate=pl.CostEstimate(flops=0, bytes_accessed=0, transcendentals=0),
    )(*arrays, *after)


def added(a, b):
    return (a.astype(F32) + b.astype(F32)).astype(BF)


def slot_of(block, y):
    return ((((block >> 1) - y) & 3) * 2 + (block >> 3)) * 2 + (block & 1)


def block_at(place, k, j):
    return ((place[0] - j) & 3) * 4 + ((place[1] - k) & 3)


def fetch(act, act_other, held, sems, order, y):
    copies = []
    for i, block in enumerate(order):
        slot = slot_of(block, y)
        pair = []
        for half, source in enumerate((act, act_other)):
            copy = pltpu.make_async_copy(source.at[slot], held.at[half, i], sems.at[half, i])
            copy.start()
            pair.append(copy)
        copies.append(pair)
    return copies


def attention_kernel(
    chunk, place, act, act_other, cot, qg, kg, weights, d_out, raw, held, held_w, sems, sems_w
):
    y = place[2]
    copies_w = []
    for block in range(16):
        copy = pltpu.make_async_copy(weights.at[block, chunk], held_w.at[block], sems_w.at[block])
        copy.start()
        copies_w.append(copy)
    copies = fetch(act, act_other, held, sems, range(16), y)
    for block in range(16):
        copies_w[block].wait()
        for half in range(2):
            copies[block][half].wait()
            part = dot(held[half, block], held_w[block], NN)
            rows = slice(half * 256, half * 256 + 256)
            if block == 0:
                raw[rows, :] = part
            else:
                raw[rows, :] += part

    factor = 1.0 / math.sqrt(HD)
    q_gain = qg[0:1, :]
    k_gain = kg[0:1, :]

    def back_norm(x_raw, inverse, gain, dy):
        gdy = gain * dy
        m = jnp.mean(x_raw * gdy, axis=-1, keepdims=True)
        return inverse * gdy - x_raw * (inverse * inverse * inverse * m)

    for p in range(8):
        a, b = slice(p * 32, p * 32 + 32), slice(256 + p * 32, 256 + p * 32 + 32)
        both = jnp.concatenate([raw[a, :], raw[b, :]], axis=0)
        q_raw, k_raw, value = both[:, 0:128], both[:, 128:256], both[:, 256:384].astype(BF)
        cols = slice(chunk * 128, chunk * 128 + 128)
        cotan = jnp.concatenate([cot[0, a, cols], cot[1, a, cols]], axis=0)
        q_inv = lax.rsqrt(jnp.mean(q_raw * q_raw, axis=-1, keepdims=True) + EPS)
        k_inv = lax.rsqrt(jnp.mean(k_raw * k_raw, axis=-1, keepdims=True) + EPS)
        q_norm = (q_raw * q_inv * q_gain).astype(BF)
        k_norm = (k_raw * k_inv * k_gain).astype(BF)
        expon = jnp.exp(dot(q_norm, k_norm, NT) * factor)
        prob = expon / jnp.sum(expon, axis=-1, keepdims=True)
        d_prob = dot(cotan, value, NT)
        d_val = dot(prob.astype(BF), cotan, TN)
        d_score = prob * (d_prob - jnp.sum(prob * d_prob, axis=-1, keepdims=True)) * factor
        d_score = d_score.astype(BF)
        d_qn = dot(d_score, k_norm, NN).astype(BF).astype(F32)
        d_kn = dot(d_score, q_norm, TN).astype(BF).astype(F32)
        d_q = back_norm(q_raw, q_inv, q_gain, d_qn).astype(BF)
        d_k = back_norm(k_raw, k_inv, k_gain, d_kn).astype(BF)
        for at, d in ((0, d_q), (128, d_k), (256, d_val.astype(BF))):
            d_out[a, at : at + 128] = d[:32]
            d_out[b, at : at + 128] = d[32:]


def term_kernel(
    place, act, act_other, d_all, back, ahead, back_late, ahead_late, here, mark, turned, held, out, sems, sems_out
):
    y = place[2]
    plan = [(back, i, k, j) for i, (k, j) in enumerate(((2, 0), (2, 1), (1, 2), (1, 3)))]
    plan += [(ahead, i, k, j) for i, (k, j) in enumerate(((2, 2), (2, 3), (3, 0), (3, 1)))]
    plan += [(back_late, j, 1, j) for j in range(2)]
    plan += [(ahead_late, j, 3, j + 2) for j in range(2)]
    plan += [(here, j, 0, j) for j in range(4)]
    copies = fetch(act, act_other, held, sems, [block_at(place, k, j) for _, _, k, j in plan], y)
    mark[...] = jnp.zeros_like(mark)
    turned[...] = d_all[...].T
    leaving = []
    for n, (ref, i, _, _) in enumerate(plan):
        for copy in copies[n]:
            copy.wait()
        total = dot(turned[:, 0:256], held[0, n], NN) + dot(turned[:, 256:512], held[1, n], NN)
        if n < 8:
            out[n] = total.astype(BF)
            copy = pltpu.make_async_copy(out.at[n], ref.at[i], sems_out.at[n])
            copy.start()
            leaving.append(copy)
        else:
            ref[i] = total.astype(BF)
    for copy in leaving:
        copy.wait()


def input_kernel(place, da, db, weights, result, held, out, sems, sems_out):
    c = place[3]
    copies = []
    for block in range(16):
        copy = pltpu.make_async_copy(weights.at[block], held.at[block], sems.at[block])
        copy.start()
        copies.append(copy)
    leaving = []
    for block in range(16):
        copies[block].wait()
        for half in range(2):
            rows = slice(half * 256, half * 256 + 256)
            total = dot(da[rows, :], held[block, 0], NT) + dot(db[rows, :], held[block, 1], NT)
            out[half, block] = total.astype(BF)
            core = c if half == 0 else 1 - c
            copy = pltpu.make_async_copy(
                out.at[half, block], result.at[core * 16 + block], sems_out.at[half, block]
            )
            copy.start()
            leaving.append(copy)
    for copy in leaving:
        copy.wait()


def call(kernel, out_shape, out_there, scratch, place, arrays, there):
    whole = pl.BlockSpec(memory_space=pltpu.VMEM)
    stay = pl.BlockSpec(memory_space=pltpu.HBM)
    return pl.pallas_call(
        kernel,
        out_shape=out_shape,
        in_specs=[pl.BlockSpec(memory_space=pltpu.SMEM)]
        + [stay if i in there else whole for i in range(len(arrays))],
        out_specs=[stay if i in out_there else whole for i in range(len(out_shape))],
        scratch_shapes=scratch,
        compiler_params=pltpu.CompilerParams(vmem_limit_bytes=20 * 2**20),
        cost_estimate=pl.CostEstimate(flops=2**20, bytes_accessed=2**10, transcendentals=0),
    )(place, *arrays)


def body(activations, w_query, w_key, w_value, q_gain, k_gain, grad_attn):
    zh, x, c, zl, y = (lax.axis_index(a) for a in ("zh", "x", "c", "zl", "y"))
    place = jnp.stack([zh, x, y, c]).astype(jnp.int32)
    cut = lax.dynamic_slice_in_dim

    def columns(core):
        return jnp.stack(
            [
                jnp.concatenate(
                    [cut(w, core * 256 + q * 128, 128, 1) for w in (w_query, w_key, w_value)], axis=1
                )
                for q in range(2)
            ]
        )

    theirs = send(columns(1 - c), "c", 1)
    ours = columns(c)
    own = jnp.concatenate(
        [jnp.where(c == 0, ours, theirs), jnp.where(c == 0, theirs, ours)], axis=1
    )
    weights = lax.all_gather(own, ("zh", "x"), axis=0)

    head = zl * 4 + y
    def exchanged(array):
        return array.reshape(2, 16, 8, 512).transpose(1, 2, 0, 3)

    def by_patches(array):
        array = lax.all_to_all(array, ("zh", "x"), 0, 0, tiled=True)
        return array.transpose(1, 0, 2, 3).reshape(256, 512)

    (mixed,) = tie([exchanged(cut(activations, head * 512, 512, 2))], [theirs])
    tokens = by_patches(mixed)
    mine = jnp.stack([tokens[:, :256], tokens[:, 256:]])
    partner = send(mine, "zl", 1)
    pair = jnp.stack([jnp.where(zl == 0, mine, partner), jnp.where(zl == 0, partner, mine)])
    one = send(pair, "y", 1)
    three = send(pair, "y", -1)
    two_a = send(one[:1], "y", 1)
    two_b = send(three[1:], "y", -1)
    act = jnp.concatenate([pair, three, two_a, two_b, one], axis=0).reshape(16, 256, 256)
    act_other = send(act, "c", 1)
    (mixed,) = tie([exchanged(grad_attn)], [partner])
    cotan = by_patches(mixed)
    cot_other = send(cut(cotan, (1 - c) * 256, 256, 1), "c", 1)
    cot = jnp.stack([cut(cotan, c * 256, 256, 1), cot_other])

    d_shape = jax.ShapeDtypeStruct((512, 384), BF)
    g_shape = [jax.ShapeDtypeStruct((n, 384, 256), BF) for n in (4, 4, 2, 2, 4)]
    g_shape.append(jax.ShapeDtypeStruct((8, 128), F32))
    gains = [jnp.stack([q_gain, q_gain]), jnp.stack([k_gain, k_gain])]

    held = pltpu.VMEM((2, 16, 256, 256), BF)
    held_sems = pltpu.SemaphoreType.DMA((2, 16))
    block_sems = pltpu.SemaphoreType.DMA((16,))

    def attention(q, gains):
        scratch = [pltpu.VMEM((512, 384), F32), held, pltpu.VMEM((16, 256, 384), BF)]
        scratch += [held_sems, block_sems]
        kernel = functools.partial(attention_kernel, q)
        arrays = (act, act_other, cot, *gains, weights)
        return call(kernel, [d_shape], (), scratch, place, arrays, (0, 1, 5))[0]

    def terms(d_all):
        scratch = [pltpu.VMEM((384, 512), BF), held, pltpu.VMEM((8, 384, 256), BF)]
        scratch += [held_sems, pltpu.SemaphoreType.DMA((8,))]
        return call(term_kernel, g_shape, (0, 1), scratch, place, (act, act_other, d_all), (0, 1))

    def input_part(d0, d1):
        scratch = [pltpu.VMEM((16, 2, 256, 384), BF), held, block_sems, held_sems]
        shape = [jax.ShapeDtypeStruct((32, 256, 256), BF)]
        return call(input_kernel, shape, (0,), scratch, place, (d0, d1, weights), (2,))[0]

    def total_of(zero, back, ahead):
        return zero.astype(F32) + back.astype(F32) + ahead.astype(F32)

    def late(g, first, axis):
        n = g[2].shape[0]
        back = send(added(g[2], first[0][:n]), axis, -1)
        ahead = send(added(g[3], first[1][:n]), axis, 1)
        return back, ahead

    def finish(g, first, second):
        n = g[2].shape[0]
        from_ahead = jnp.concatenate([second[0], first[0][n:]], axis=0)
        from_behind = jnp.concatenate([first[1][n:], second[1]], axis=0)
        return total_of(g[4], from_ahead, from_behind)

    def early(g, axis):
        return send(g[0], axis, -1), send(g[1], axis, 1)

    def split_z(s):
        half = s.shape[1] // 2
        back = jnp.concatenate([s[2, :half], s[1, half:]], axis=0)
        ahead = jnp.concatenate([s[2, half:], s[3, :half]], axis=0)
        return [back, ahead, s[1, :half], s[3, half:], s[0]]

    d0 = attention(0, gains)
    g_0 = terms(d0)
    x_early_0 = early(g_0, "x")
    d1 = attention(1, tie(gains, [g_0[5]]))
    part = input_part(d0, d1)
    g_1 = list(terms(d1))
    on = tie([part, g_1[0], g_1[1]], [a[0, :16, :128] for a in x_early_0])
    part, g_1[0], g_1[1] = on
    result = lax.psum_scatter(part, ("c", "zl", "y"), scatter_dimension=0, tiled=True)
    x_late_0 = late(g_0, x_early_0, "x")
    x_early_1 = early(g_1, "x")
    s_0 = split_z(finish(g_0, x_early_0, x_late_0).astype(BF))
    z_early_0 = early(s_0, "zh")
    x_late_1 = late(g_1, x_early_1, "x")

    z_late_0 = late(s_0, z_early_0, "zh")

    result = result.reshape(2, 8, 16, 2, 256).transpose(2, 1, 3, 0, 4).reshape(16, 8, 2, 512)
    result = lax.all_to_all(result, ("zh", "x"), 0, 0, tiled=True)
    grad_input = result.reshape(128, 2, 512).transpose(1, 0, 2)

    s_1 = split_z(finish(g_1, x_early_1, x_late_1).astype(BF))
    z_early_1 = early(s_1, "zh")
    late_operands = [added(s_1[2], z_early_1[0][:192]), added(s_1[3], z_early_1[1][:192])]
    late_operands = tie(late_operands, [result])
    z_late_1 = (send(late_operands[0], "zh", -1), send(late_operands[1], "zh", 1))

    both = jnp.stack([finish(s_0, z_early_0, z_late_0), finish(s_1, z_early_1, z_late_1)])
    kept = cut(both, c * 128, 128, 2)
    other = send(cut(both, (1 - c) * 128, 128, 2).astype(BF), "c", 1).astype(F32)
    heads = jnp.concatenate([jnp.where(c == 0, kept, other), jnp.where(c == 0, other, kept)], axis=0)
    heads = heads.reshape(4, 3, 128, 128).transpose(1, 3, 0, 2).reshape(3, 128, 512)
    return (grad_input, heads[0], heads[1], heads[2])


def solution(mesh):
    fine = Mesh(mesh.devices.reshape(4, 4, 2, 2, 4), ("zh", "x", "c", "zl", "y"))
    frame = ("zh", "x", "c")
    head = ("zl", "y")
    weight = P(frame, head)
    return jax.shard_map(
        body,
        mesh=fine,
        in_specs=(P(frame, None, None), weight, weight, weight, P(), P(), P(frame, None, head)),
        out_specs=(P(frame, None, head), weight, weight, weight),
        check_vma=False,
    )
```

```python
import functools
import math

import jax
import jax.numpy as jnp
from jax import lax
from jax.experimental import pallas as pl
from jax.experimental.pallas import tpu as pltpu
from jax.sharding import Mesh, PartitionSpec as P

HD = 128
EPS = 1e-06
BF = jnp.bfloat16
F32 = jnp.float32
NT = (((1,), (1,)), ((), ()))
TN = (((0,), (0,)), ((), ()))
NN = (((1,), (0,)), ((), ()))
dot = functools.partial(lax.dot_general, preferred_element_type=F32)


def send(array, axis, shift):
    n = lax.axis_size(axis)
    return lax.ppermute(array, axis, [(i, (i + shift) % n) for i in range(n)])


def nothing(*refs):
    pass


def tie(arrays, after):
    where = pl.BlockSpec(memory_space=pl.ANY)
    return pl.pallas_call(
        nothing,
        out_shape=[jax.ShapeDtypeStruct(a.shape, a.dtype) for a in arrays],
        in_specs=[where] * (len(arrays) + len(after)),
        out_specs=[where] * len(arrays),
        input_output_aliases={i: i for i in range(len(arrays))},
        cost_estimate=pl.CostEstimate(flops=0, bytes_accessed=0, transcendentals=0),
    )(*arrays, *after)


def added(a, b):
    return (a.astype(F32) + b.astype(F32)).astype(BF)


def slot_of(block, y):
    return ((((block >> 1) - y) & 3) * 2 + (block >> 3)) * 2 + (block & 1)


def block_at(place, k, j):
    return ((place[0] - j) & 3) * 4 + ((place[1] - k) & 3)


def attention(chunk, place, act, act_other, cot, qg, kg, weights, d_out, raw):
    y = place[2]
    for block in range(16):
        for half, held in enumerate((act, act_other)):
            part = dot(held[slot_of(block, y)], weights[block, chunk], NN)
            rows = slice(half * 256, half * 256 + 256)
            if block == 0:
                raw[rows, :] = part
            else:
                raw[rows, :] += part

    factor = 1.0 / math.sqrt(HD)
    q_gain = qg[0:1, :]
    k_gain = kg[0:1, :]

    def back_norm(x_raw, inverse, gain, dy):
        gdy = gain * dy
        m = jnp.mean(x_raw * gdy, axis=-1, keepdims=True)
        return inverse * gdy - x_raw * (inverse * inverse * inverse * m)

    for p in range(8):
        a, b = slice(p * 32, p * 32 + 32), slice(256 + p * 32, 256 + p * 32 + 32)
        both = jnp.concatenate([raw[a, :], raw[b, :]], axis=0)
        q_raw, k_raw, value = both[:, 0:128], both[:, 128:256], both[:, 256:384].astype(BF)
        cols = slice(chunk * 128, chunk * 128 + 128)
        cotan = jnp.concatenate([cot[0, a, cols], cot[1, a, cols]], axis=0)
        q_inv = lax.rsqrt(jnp.mean(q_raw * q_raw, axis=-1, keepdims=True) + EPS)
        k_inv = lax.rsqrt(jnp.mean(k_raw * k_raw, axis=-1, keepdims=True) + EPS)
        q_norm = (q_raw * q_inv * q_gain).astype(BF)
        k_norm = (k_raw * k_inv * k_gain).astype(BF)
        expon = jnp.exp(dot(q_norm, k_norm, NT) * factor)
        prob = expon / jnp.sum(expon, axis=-1, keepdims=True)
        d_prob = dot(cotan, value, NT)
        d_val = dot(prob.astype(BF), cotan, TN)
        d_score = prob * (d_prob - jnp.sum(prob * d_prob, axis=-1, keepdims=True)) * factor
        d_score = d_score.astype(BF)
        d_qn = dot(d_score, k_norm, NN).astype(BF).astype(F32)
        d_kn = dot(d_score, q_norm, TN).astype(BF).astype(F32)
        d_q = back_norm(q_raw, q_inv, q_gain, d_qn).astype(BF)
        d_k = back_norm(k_raw, k_inv, k_gain, d_kn).astype(BF)
        for at, d in ((0, d_q), (128, d_k), (256, d_val.astype(BF))):
            d_out[a, at : at + 128] = d[:32]
            d_out[b, at : at + 128] = d[32:]


def terms(place, act, act_other, d_all, back, ahead, back_late, ahead_late, here, turned):
    y = place[2]
    turned[...] = d_all[...].T
    plan = [(back, i, k, j) for i, (k, j) in enumerate(((2, 0), (2, 1), (1, 2), (1, 3)))]
    plan += [(ahead, i, k, j) for i, (k, j) in enumerate(((2, 2), (2, 3), (3, 0), (3, 1)))]
    plan += [(back_late, j, 1, j) for j in range(2)]
    plan += [(ahead_late, j, 3, j + 2) for j in range(2)]
    plan += [(here, j, 0, j) for j in range(4)]
    for ref, i, k, j in plan:
        slot = slot_of(block_at(place, k, j), y)
        total = dot(turned[:, 0:256], act[slot], NN) + dot(turned[:, 256:512], act_other[slot], NN)
        ref[i] = total.astype(BF)


def first_kernel(
    place, act, act_other, cot, qg, kg, weights, d_out, back, ahead, back_late, ahead_late, here, mark, raw, turned
):
    mark[...] = jnp.zeros_like(mark)
    attention(0, place, act, act_other, cot, qg, kg, weights, d_out, raw)
    terms(place, act, act_other, d_out, back, ahead, back_late, ahead_late, here, turned)


def second_kernel(
    place, act, act_other, cot, qg, kg, weights, da, near, far_0, far_1, far_2, far_3, back, ahead, back_late, ahead_late, here, db, raw, turned
):
    attention(1, place, act, act_other, cot, qg, kg, weights, db, raw)
    for block in range(16):
        for half in range(2):
            rows = slice(half * 256, half * 256 + 256)
            total = dot(da[rows, :], weights[block, 0], NT)
            total += dot(db[rows, :], weights[block, 1], NT)
            if half == 0:
                near[block] = total.astype(BF)
            else:
                (far_0, far_1, far_2, far_3)[block // 4][block % 4] = total.astype(BF)
    terms(place, act, act_other, db, back, ahead, back_late, ahead_late, here, turned)


def call(kernel, out_shape, scratch, place, *arrays):
    whole = pl.BlockSpec(memory_space=pltpu.VMEM)
    return pl.pallas_call(
        kernel,
        out_shape=out_shape,
        in_specs=[pl.BlockSpec(memory_space=pltpu.SMEM)] + [whole] * len(arrays),
        out_specs=jax.tree.map(lambda _: whole, out_shape),
        scratch_shapes=scratch,
        compiler_params=pltpu.CompilerParams(vmem_limit_bytes=16 * 2**20),
        cost_estimate=pl.CostEstimate(flops=2**20, bytes_accessed=2**10, transcendentals=0),
    )(place, *arrays)


def body(activations, w_query, w_key, w_value, q_gain, k_gain, grad_attn):
    zh, x, c, zl, y = (lax.axis_index(a) for a in ("zh", "x", "c", "zl", "y"))
    place = jnp.stack([zh, x, y]).astype(jnp.int32)
    cut = lax.dynamic_slice_in_dim

    def columns(core):
        return jnp.stack(
            [
                jnp.concatenate(
                    [cut(w, core * 256 + q * 128, 128, 1) for w in (w_query, w_key, w_value)], axis=1
                )
                for q in range(2)
            ]
        )

    theirs = send(columns(1 - c), "c", 1)
    ours = columns(c)
    own = jnp.concatenate(
        [jnp.where(c == 0, ours, theirs), jnp.where(c == 0, theirs, ours)], axis=1
    )
    weights = lax.all_gather(own, ("zh", "x"), axis=0)

    head = zl * 4 + y
    mixed = jnp.concatenate([cut(activations, head * 512, 512, 2), grad_attn], axis=2)
    mixed = mixed.reshape(2, 16, 8, 1024).transpose(1, 2, 0, 3)

    (mixed,) = tie([mixed], [theirs])
    mixed = lax.all_to_all(mixed, ("zh", "x"), 0, 0, tiled=True)
    tokens = mixed.transpose(1, 0, 2, 3).reshape(256, 1024)
    mine = jnp.stack([tokens[:, :256], tokens[:, 256:512]])
    cot_own = cut(tokens, 512 + c * 256, 256, 1)
    cot_other = send(cut(tokens, 512 + (1 - c) * 256, 256, 1), "c", 1)
    cot = jnp.stack([cot_own, cot_other])
    partner = send(mine, "zl", 1)
    pair = jnp.stack([jnp.where(zl == 0, mine, partner), jnp.where(zl == 0, partner, mine)])
    one = send(pair, "y", 1)
    three = send(pair, "y", -1)
    two_a = send(one[:1], "y", 1)
    two_b = send(three[1:], "y", -1)
    act = jnp.concatenate([pair, three, two_a, two_b, one], axis=0).reshape(16, 256, 256)
    act_other = send(act, "c", 1)

    d_shape = jax.ShapeDtypeStruct((512, 384), BF)
    g_shape = [jax.ShapeDtypeStruct((n, 384, 256), BF) for n in (4, 4, 2, 2, 4)]
    part_shape = [jax.ShapeDtypeStruct((n, 256, 256), BF) for n in (16, 4, 4, 4, 4)]
    mark_shape = jax.ShapeDtypeStruct((8, 128), F32)
    gains = [jnp.stack([q_gain, q_gain]), jnp.stack([k_gain, k_gain])]
    scratch = [pltpu.VMEM((512, 384), F32), pltpu.VMEM((384, 512), BF)]
    arrays = (act, act_other, cot)

    def total_of(zero, back, ahead):
        return zero.astype(F32) + back.astype(F32) + ahead.astype(F32)

    def late(g, first, axis):
        n = g[2].shape[0]
        back = send(added(g[2], first[0][:n]), axis, -1)
        ahead = send(added(g[3], first[1][:n]), axis, 1)
        return back, ahead

    def finish(g, first, second):
        n = g[2].shape[0]
        from_ahead = jnp.concatenate([second[0], first[0][n:]], axis=0)
        from_behind = jnp.concatenate([first[1][n:], second[1]], axis=0)
        return total_of(g[4], from_ahead, from_behind)

    def early(g, axis):
        return send(g[0], axis, -1), send(g[1], axis, 1)

    def split_z(s):
        half = s.shape[1] // 2
        back = jnp.concatenate([s[2, :half], s[1, half:]], axis=0)
        ahead = jnp.concatenate([s[2, half:], s[3, :half]], axis=0)
        return [back, ahead, s[1, :half], s[3, half:], s[0]]

    d0, *g_0, mark = call(
        first_kernel, [d_shape, *g_shape, mark_shape], scratch, place, *arrays, *gains, weights
    )
    x_early_0 = early(g_0, "x")
    gains = tie(gains, [mark])
    part, *outs = call(
        second_kernel,
        [*part_shape, *g_shape],
        [pltpu.VMEM((512, 384), BF), *scratch],
        place,
        *arrays,
        *gains,
        weights,
        d0,
    )
    got = jnp.concatenate([send(far, "c", 1) for far in outs[:4]], axis=0)
    g_1 = outs[4:]
    x_late_0 = late(g_0, x_early_0, "x")
    on = tie([part, *g_1[:2]], [a[0, :16, :128] for a in x_early_0])
    part, g_1[0], g_1[1] = on
    x_early_1 = early(g_1, "x")

    part = added(part, got)
    result = lax.psum_scatter(part, ("zl", "y"), scatter_dimension=0, tiled=True)

    s_0 = split_z(finish(g_0, x_early_0, x_late_0).astype(BF))
    z_early_0 = early(s_0, "zh")
    x_late_1 = late(g_1, x_early_1, "x")

    z_late_0 = late(s_0, z_early_0, "zh")

    result = result.reshape(2, 8, 16, 2, 256).transpose(2, 1, 3, 0, 4).reshape(16, 8, 2, 512)
    result = lax.all_to_all(result, ("zh", "x"), 0, 0, tiled=True)
    grad_input = result.reshape(128, 2, 512).transpose(1, 0, 2)

    s_1 = split_z(finish(g_1, x_early_1, x_late_1).astype(BF))
    z_early_1 = early(s_1, "zh")
    late_operands = [added(s_1[2], z_early_1[0][:192]), added(s_1[3], z_early_1[1][:192])]
    late_operands = tie(late_operands, [result])
    z_late_1 = (send(late_operands[0], "zh", -1), send(late_operands[1], "zh", 1))

    both = jnp.stack([finish(s_0, z_early_0, z_late_0), finish(s_1, z_early_1, z_late_1)])
    kept = cut(both, c * 128, 128, 2)
    other = send(cut(both, (1 - c) * 128, 128, 2).astype(BF), "c", 1).astype(F32)
    heads = jnp.concatenate([jnp.where(c == 0, kept, other), jnp.where(c == 0, other, kept)], axis=0)
    heads = heads.reshape(4, 3, 128, 128).transpose(1, 3, 0, 2).reshape(3, 128, 512)
    return (grad_input, heads[0], heads[1], heads[2])


def solution(mesh):
    fine = Mesh(mesh.devices.reshape(4, 4, 2, 2, 4), ("zh", "x", "c", "zl", "y"))
    frame = ("zh", "x", "c")
    head = ("zl", "y")
    weight = P(frame, head)
    return jax.shard_map(
        body,
        mesh=fine,
        in_specs=(P(frame, None, None), weight, weight, weight, P(), P(), P(frame, None, head)),
        out_specs=(P(frame, None, head), weight, weight, weight),
        check_vma=False,
    )
```

```python
import functools
import math

import jax
import jax.numpy as jnp
from jax import lax
from jax.experimental import pallas as pl
from jax.experimental.pallas import tpu as pltpu
from jax.sharding import Mesh, PartitionSpec as P

HD = 128
EPS = 1e-06
BF = jnp.bfloat16
F32 = jnp.float32
NT = (((1,), (1,)), ((), ()))
TN = (((0,), (0,)), ((), ()))
NN = (((1,), (0,)), ((), ()))
dot = functools.partial(lax.dot_general, preferred_element_type=F32)


def send(array, axis, shift):
    n = lax.axis_size(axis)
    return lax.ppermute(array, axis, [(i, (i + shift) % n) for i in range(n)])


def nothing(*refs):
    pass


def tie(arrays, after):
    where = pl.BlockSpec(memory_space=pl.ANY)
    return pl.pallas_call(
        nothing,
        out_shape=[jax.ShapeDtypeStruct(a.shape, a.dtype) for a in arrays],
        in_specs=[where] * (len(arrays) + len(after)),
        out_specs=[where] * len(arrays),
        input_output_aliases={i: i for i in range(len(arrays))},
        cost_estimate=pl.CostEstimate(flops=0, bytes_accessed=0, transcendentals=0),
    )(*arrays, *after)


def added(a, b):
    return (a.astype(F32) + b.astype(F32)).astype(BF)


def slot_of(block, y):
    return ((((block >> 1) - y) & 3) * 2 + (block >> 3)) * 2 + (block & 1)


def block_at(place, k, j):
    return ((place[0] - j) & 3) * 4 + ((place[1] - k) & 3)


def attention(chunk, place, act, act_other, cot, qg, kg, weights, d_out, raw):
    y = place[2]
    for block in range(16):
        for half, held in enumerate((act, act_other)):
            part = dot(held[slot_of(block, y)], weights[block, chunk], NN)
            rows = slice(half * 256, half * 256 + 256)
            if block == 0:
                raw[rows, :] = part
            else:
                raw[rows, :] += part

    factor = 1.0 / math.sqrt(HD)
    q_gain = qg[0:1, :]
    k_gain = kg[0:1, :]

    def back_norm(x_raw, inverse, gain, dy):
        gdy = gain * dy
        m = jnp.mean(x_raw * gdy, axis=-1, keepdims=True)
        return inverse * gdy - x_raw * (inverse * inverse * inverse * m)

    for p in range(8):
        a, b = slice(p * 32, p * 32 + 32), slice(256 + p * 32, 256 + p * 32 + 32)
        both = jnp.concatenate([raw[a, :], raw[b, :]], axis=0)
        q_raw, k_raw, value = both[:, 0:128], both[:, 128:256], both[:, 256:384].astype(BF)
        cols = slice(chunk * 128, chunk * 128 + 128)
        cotan = jnp.concatenate([cot[0, a, cols], cot[1, a, cols]], axis=0)
        q_inv = lax.rsqrt(jnp.mean(q_raw * q_raw, axis=-1, keepdims=True) + EPS)
        k_inv = lax.rsqrt(jnp.mean(k_raw * k_raw, axis=-1, keepdims=True) + EPS)
        q_norm = (q_raw * q_inv * q_gain).astype(BF)
        k_norm = (k_raw * k_inv * k_gain).astype(BF)
        expon = jnp.exp(dot(q_norm, k_norm, NT) * factor)
        prob = expon / jnp.sum(expon, axis=-1, keepdims=True)
        d_prob = dot(cotan, value, NT)
        d_val = dot(prob.astype(BF), cotan, TN)
        d_score = prob * (d_prob - jnp.sum(prob * d_prob, axis=-1, keepdims=True)) * factor
        d_score = d_score.astype(BF)
        d_qn = dot(d_score, k_norm, NN).astype(BF).astype(F32)
        d_kn = dot(d_score, q_norm, TN).astype(BF).astype(F32)
        d_q = back_norm(q_raw, q_inv, q_gain, d_qn).astype(BF)
        d_k = back_norm(k_raw, k_inv, k_gain, d_kn).astype(BF)
        for at, d in ((0, d_q), (128, d_k), (256, d_val.astype(BF))):
            d_out[a, at : at + 128] = d[:32]
            d_out[b, at : at + 128] = d[32:]


def terms(place, act, act_other, d_all, back, ahead, back_late, ahead_late, here, turned):
    y = place[2]
    turned[...] = d_all[...].T
    plan = [(back, i, k, j) for i, (k, j) in enumerate(((2, 0), (2, 1), (1, 2), (1, 3)))]
    plan += [(ahead, i, k, j) for i, (k, j) in enumerate(((2, 2), (2, 3), (3, 0), (3, 1)))]
    plan += [(back_late, j, 1, j) for j in range(2)]
    plan += [(ahead_late, j, 3, j + 2) for j in range(2)]
    plan += [(here, j, 0, j) for j in range(4)]
    for ref, i, k, j in plan:
        slot = slot_of(block_at(place, k, j), y)
        total = dot(turned[:, 0:256], act[slot], NN) + dot(turned[:, 256:512], act_other[slot], NN)
        ref[i] = total.astype(BF)


def first_kernel(
    place, act, act_other, cot, qg, kg, weights, d_out, back, ahead, back_late, ahead_late, here, mark, raw, turned
):
    mark[...] = jnp.zeros_like(mark)
    attention(0, place, act, act_other, cot, qg, kg, weights, d_out, raw)
    terms(place, act, act_other, d_out, back, ahead, back_late, ahead_late, here, turned)


def second_kernel(
    place, act, act_other, cot, qg, kg, weights, da, near, far_0, far_1, far_2, far_3, back, ahead, back_late, ahead_late, here, db, raw, turned
):
    attention(1, place, act, act_other, cot, qg, kg, weights, db, raw)
    for block in range(16):
        for half in range(2):
            rows = slice(half * 256, half * 256 + 256)
            total = dot(da[rows, :], weights[block, 0], NT)
            total += dot(db[rows, :], weights[block, 1], NT)
            if half == 0:
                near[block] = total.astype(BF)
            else:
                (far_0, far_1, far_2, far_3)[block // 4][block % 4] = total.astype(BF)
    terms(place, act, act_other, db, back, ahead, back_late, ahead_late, here, turned)


def call(kernel, out_shape, scratch, place, *arrays):
    whole = pl.BlockSpec(memory_space=pltpu.VMEM)
    return pl.pallas_call(
        kernel,
        out_shape=out_shape,
        in_specs=[pl.BlockSpec(memory_space=pltpu.SMEM)] + [whole] * len(arrays),
        out_specs=jax.tree.map(lambda _: whole, out_shape),
        scratch_shapes=scratch,
        compiler_params=pltpu.CompilerParams(vmem_limit_bytes=16 * 2**20),
        cost_estimate=pl.CostEstimate(flops=2**20, bytes_accessed=2**10, transcendentals=0),
    )(place, *arrays)


def body(activations, w_query, w_key, w_value, q_gain, k_gain, grad_attn):
    zh, x, c, zl, y = (lax.axis_index(a) for a in ("zh", "x", "c", "zl", "y"))
    place = jnp.stack([zh, x, y]).astype(jnp.int32)
    cut = lax.dynamic_slice_in_dim

    def columns(core):
        return jnp.stack(
            [
                jnp.concatenate(
                    [cut(w, core * 256 + q * 128, 128, 1) for w in (w_query, w_key, w_value)], axis=1
                )
                for q in range(2)
            ]
        )

    theirs = send(columns(1 - c), "c", 1)
    ours = columns(c)
    own = jnp.concatenate(
        [jnp.where(c == 0, ours, theirs), jnp.where(c == 0, theirs, ours)], axis=1
    )
    weights = lax.all_gather(own, ("zh", "x"), axis=0)

    head = zl * 4 + y
    mixed = jnp.concatenate([cut(activations, head * 512, 512, 2), grad_attn], axis=2)
    mixed = mixed.reshape(2, 16, 8, 1024).transpose(1, 2, 0, 3)

    (mixed,) = tie([mixed], [theirs])
    mixed = lax.all_to_all(mixed, ("zh", "x"), 0, 0, tiled=True)
    tokens = mixed.transpose(1, 0, 2, 3).reshape(256, 1024)
    mine = jnp.stack([tokens[:, :256], tokens[:, 256:512]])
    cot_own = cut(tokens, 512 + c * 256, 256, 1)
    cot_other = send(cut(tokens, 512 + (1 - c) * 256, 256, 1), "c", 1)
    cot = jnp.stack([cot_own, cot_other])
    partner = send(mine, "zl", 1)
    pair = jnp.stack([jnp.where(zl == 0, mine, partner), jnp.where(zl == 0, partner, mine)])
    one = send(pair, "y", 1)
    three = send(pair, "y", -1)
    two_a = send(one[:1], "y", 1)
    two_b = send(three[1:], "y", -1)
    act = jnp.concatenate([pair, three, two_a, two_b, one], axis=0).reshape(16, 256, 256)
    act_other = send(act, "c", 1)

    d_shape = jax.ShapeDtypeStruct((512, 384), BF)
    g_shape = [jax.ShapeDtypeStruct((n, 384, 256), BF) for n in (4, 4, 2, 2, 4)]
    part_shape = [jax.ShapeDtypeStruct((n, 256, 256), BF) for n in (16, 4, 4, 4, 4)]
    mark_shape = jax.ShapeDtypeStruct((8, 128), F32)
    gains = [jnp.stack([q_gain, q_gain]), jnp.stack([k_gain, k_gain])]
    scratch = [pltpu.VMEM((512, 384), F32), pltpu.VMEM((384, 512), BF)]
    arrays = (act, act_other, cot)

    def total_of(zero, back, ahead):
        return zero.astype(F32) + back.astype(F32) + ahead.astype(F32)

    def late(g, first, axis):
        n = g[2].shape[0]
        back = send(added(g[2], first[0][:n]), axis, -1)
        ahead = send(added(g[3], first[1][:n]), axis, 1)
        return back, ahead

    def finish(g, first, second):
        n = g[2].shape[0]
        from_ahead = jnp.concatenate([second[0], first[0][n:]], axis=0)
        from_behind = jnp.concatenate([first[1][n:], second[1]], axis=0)
        return total_of(g[4], from_ahead, from_behind)

    def early(g, axis):
        return send(g[0], axis, -1), send(g[1], axis, 1)

    def split_z(s):
        half = s.shape[1] // 2
        back = jnp.concatenate([s[2, :half], s[1, half:]], axis=0)
        ahead = jnp.concatenate([s[2, half:], s[3, :half]], axis=0)
        return [back, ahead, s[1, :half], s[3, half:], s[0]]

    d0, *g_0, mark = call(
        first_kernel, [d_shape, *g_shape, mark_shape], scratch, place, *arrays, *gains, weights
    )
    x_early_0 = early(g_0, "x")
    gains = tie(gains, [mark])
    part, *outs = call(
        second_kernel,
        [*part_shape, *g_shape],
        [pltpu.VMEM((512, 384), BF), *scratch],
        place,
        *arrays,
        *gains,
        weights,
        d0,
    )
    got = jnp.concatenate([send(far, "c", 1) for far in outs[:4]], axis=0)
    g_1 = outs[4:]
    x_late_0 = late(g_0, x_early_0, "x")
    on = tie([part, *g_1[:2]], x_early_0)
    part, g_1[0], g_1[1] = on
    x_early_1 = early(g_1, "x")

    part = added(part, got)
    result = lax.psum_scatter(part, ("zl", "y"), scatter_dimension=0, tiled=True)

    s_0 = split_z(finish(g_0, x_early_0, x_late_0).astype(BF))
    z_early_0 = early(s_0, "zh")
    x_late_1 = late(g_1, x_early_1, "x")

    operands = [added(s_0[2], z_early_0[0][:192]), added(s_0[3], z_early_0[1][:192])]
    operands = tie(operands, x_early_1)
    z_late_0 = (send(operands[0], "zh", -1), send(operands[1], "zh", 1))

    result = result.reshape(2, 8, 16, 2, 256).transpose(2, 1, 3, 0, 4).reshape(16, 8, 2, 512)
    result = lax.all_to_all(result, ("zh", "x"), 0, 0, tiled=True)
    grad_input = result.reshape(128, 2, 512).transpose(1, 0, 2)

    s_1 = split_z(finish(g_1, x_early_1, x_late_1).astype(BF))
    z_early_1 = early(s_1, "zh")
    z_late_1 = late(s_1, z_early_1, "zh")

    both = jnp.stack([finish(s_0, z_early_0, z_late_0), finish(s_1, z_early_1, z_late_1)])
    kept = cut(both, c * 128, 128, 2)
    (away,) = tie([cut(both, (1 - c) * 128, 128, 2).astype(BF)], [result])
    other = send(away, "c", 1).astype(F32)
    heads = jnp.concatenate([jnp.where(c == 0, kept, other), jnp.where(c == 0, other, kept)], axis=0)
    heads = heads.reshape(4, 3, 128, 128).transpose(1, 3, 0, 2).reshape(3, 128, 512)
    return (grad_input, heads[0], heads[1], heads[2])


def solution(mesh):
    fine = Mesh(mesh.devices.reshape(4, 4, 2, 2, 4), ("zh", "x", "c", "zl", "y"))
    frame = ("zh", "x", "c")
    head = ("zl", "y")
    weight = P(frame, head)
    return jax.shard_map(
        body,
        mesh=fine,
        in_specs=(P(frame, None, None), weight, weight, weight, P(), P(), P(frame, None, head)),
        out_specs=(P(frame, None, head), weight, weight, weight),
        check_vma=False,
    )
```

```python
import functools
import math

import jax
import jax.numpy as jnp
from jax import lax
from jax.experimental import pallas as pl
from jax.experimental.pallas import tpu as pltpu
from jax.sharding import Mesh, PartitionSpec as P

HD = 128
EPS = 1e-06
BF = jnp.bfloat16
F32 = jnp.float32
NT = (((1,), (1,)), ((), ()))
TN = (((0,), (0,)), ((), ()))
NN = (((1,), (0,)), ((), ()))
dot = functools.partial(lax.dot_general, preferred_element_type=F32)


def send(array, axis, shift):
    n = lax.axis_size(axis)
    return lax.ppermute(array, axis, [(i, (i + shift) % n) for i in range(n)])


def nothing(*refs):
    pass


def tie(arrays, after):
    where = pl.BlockSpec(memory_space=pl.ANY)
    return pl.pallas_call(
        nothing,
        out_shape=[jax.ShapeDtypeStruct(a.shape, a.dtype) for a in arrays],
        in_specs=[where] * (len(arrays) + len(after)),
        out_specs=[where] * len(arrays),
        input_output_aliases={i: i for i in range(len(arrays))},
        cost_estimate=pl.CostEstimate(flops=0, bytes_accessed=0, transcendentals=0),
    )(*arrays, *after)


def added(a, b):
    return (a.astype(F32) + b.astype(F32)).astype(BF)


def slot_of(block, y):
    return ((((block >> 1) - y) & 3) * 2 + (block >> 3)) * 2 + (block & 1)


def block_at(place, k, j):
    return ((place[0] - j) & 3) * 4 + ((place[1] - k) & 3)


def attention(chunk, place, act, act_other, cot, qg, kg, weights, d_out, raw):
    y = place[2]
    for half, held in enumerate((act, act_other)):
        rows = slice(half * 256, half * 256 + 256)
        for first in range(0, 16, 4):
            part = dot(held[slot_of(first, y)], weights[first, chunk], NN)
            for block in range(first + 1, first + 4):
                part += dot(held[slot_of(block, y)], weights[block, chunk], NN)
            if first == 0:
                raw[rows, :] = part
            else:
                raw[rows, :] += part

    factor = 1.0 / math.sqrt(HD)
    q_gain = qg[0:1, :]
    k_gain = kg[0:1, :]

    def back_norm(x_raw, inverse, gain, dy):
        gdy = gain * dy
        m = jnp.mean(x_raw * gdy, axis=-1, keepdims=True)
        return inverse * gdy - x_raw * (inverse * inverse * inverse * m)

    for p in range(8):
        a, b = slice(p * 32, p * 32 + 32), slice(256 + p * 32, 256 + p * 32 + 32)
        both = jnp.concatenate([raw[a, :], raw[b, :]], axis=0)
        q_raw, k_raw, value = both[:, 0:128], both[:, 128:256], both[:, 256:384].astype(BF)
        cols = slice(chunk * 128, chunk * 128 + 128)
        cotan = jnp.concatenate([cot[0, a, cols], cot[1, a, cols]], axis=0)
        q_inv = lax.rsqrt(jnp.mean(q_raw * q_raw, axis=-1, keepdims=True) + EPS)
        k_inv = lax.rsqrt(jnp.mean(k_raw * k_raw, axis=-1, keepdims=True) + EPS)
        q_norm = (q_raw * q_inv * q_gain).astype(BF)
        k_norm = (k_raw * k_inv * k_gain).astype(BF)
        expon = jnp.exp(dot(q_norm, k_norm, NT) * factor)
        prob = expon / jnp.sum(expon, axis=-1, keepdims=True)
        d_prob = dot(cotan, value, NT)
        d_val = dot(prob.astype(BF), cotan, TN)
        d_score = prob * (d_prob - jnp.sum(prob * d_prob, axis=-1, keepdims=True)) * factor
        d_score = d_score.astype(BF)
        d_qn = dot(d_score, k_norm, NN).astype(BF).astype(F32)
        d_kn = dot(d_score, q_norm, TN).astype(BF).astype(F32)
        d_q = back_norm(q_raw, q_inv, q_gain, d_qn).astype(BF)
        d_k = back_norm(k_raw, k_inv, k_gain, d_kn).astype(BF)
        for at, d in ((0, d_q), (128, d_k), (256, d_val.astype(BF))):
            d_out[a, at : at + 128] = d[:32]
            d_out[b, at : at + 128] = d[32:]


def terms(place, act, act_other, d_all, back, ahead, back_late, ahead_late, here, turned):
    y = place[2]
    turned[...] = d_all[...].T
    plan = [(back, i, k, j) for i, (k, j) in enumerate(((2, 0), (2, 1), (1, 2), (1, 3)))]
    plan += [(ahead, i, k, j) for i, (k, j) in enumerate(((2, 2), (2, 3), (3, 0), (3, 1)))]
    plan += [(back_late, j, 1, j) for j in range(2)]
    plan += [(ahead_late, j, 3, j + 2) for j in range(2)]
    plan += [(here, j, 0, j) for j in range(4)]
    for ref, i, k, j in plan:
        slot = slot_of(block_at(place, k, j), y)
        total = dot(turned[:, 0:256], act[slot], NN) + dot(turned[:, 256:512], act_other[slot], NN)
        ref[i] = total.astype(BF)


def first_kernel(
    place, act, act_other, cot, qg, kg, weights, d_out, back, ahead, back_late, ahead_late, here, mark, raw, turned
):
    mark[...] = jnp.zeros_like(mark)
    attention(0, place, act, act_other, cot, qg, kg, weights, d_out, raw)
    terms(place, act, act_other, d_out, back, ahead, back_late, ahead_late, here, turned)


def second_kernel(
    place, act, act_other, cot, qg, kg, weights, da, near, far_0, far_1, far_2, far_3, back, ahead, back_late, ahead_late, here, db, raw, turned
):
    attention(1, place, act, act_other, cot, qg, kg, weights, db, raw)
    for block in range(16):
        for half in range(2):
            rows = slice(half * 256, half * 256 + 256)
            total = dot(da[rows, :], weights[block, 0], NT)
            total += dot(db[rows, :], weights[block, 1], NT)
            if half == 0:
                near[block] = total.astype(BF)
            else:
                (far_0, far_1, far_2, far_3)[block // 4][block % 4] = total.astype(BF)
    terms(place, act, act_other, db, back, ahead, back_late, ahead_late, here, turned)


def call(kernel, out_shape, scratch, place, *arrays):
    whole = pl.BlockSpec(memory_space=pltpu.VMEM)
    return pl.pallas_call(
        kernel,
        out_shape=out_shape,
        in_specs=[pl.BlockSpec(memory_space=pltpu.SMEM)] + [whole] * len(arrays),
        out_specs=jax.tree.map(lambda _: whole, out_shape),
        scratch_shapes=scratch,
        compiler_params=pltpu.CompilerParams(vmem_limit_bytes=54 * 2**20),
        cost_estimate=pl.CostEstimate(flops=2**20, bytes_accessed=2**10, transcendentals=0),
    )(place, *arrays)


def body(activations, w_query, w_key, w_value, q_gain, k_gain, grad_attn):
    zh, x, c, zl, y = (lax.axis_index(a) for a in ("zh", "x", "c", "zl", "y"))
    place = jnp.stack([zh, x, y]).astype(jnp.int32)
    cut = lax.dynamic_slice_in_dim

    def columns(core):
        return jnp.stack(
            [
                jnp.concatenate(
                    [cut(w, core * 256 + q * 128, 128, 1) for w in (w_query, w_key, w_value)], axis=1
                )
                for q in range(2)
            ]
        )

    theirs = send(columns(1 - c), "c", 1)
    ours = columns(c)
    own = jnp.concatenate(
        [jnp.where(c == 0, ours, theirs), jnp.where(c == 0, theirs, ours)], axis=1
    )
    weights = lax.all_gather(own, ("zh", "x"), axis=0)

    head = zl * 4 + y
    mixed = jnp.concatenate([cut(activations, head * 512, 512, 2), grad_attn], axis=2)
    mixed = mixed.reshape(2, 16, 8, 1024).transpose(1, 2, 0, 3)

    (mixed,) = tie([mixed], [theirs])
    mixed = lax.all_to_all(mixed, ("zh", "x"), 0, 0, tiled=True)
    tokens = mixed.transpose(1, 0, 2, 3).reshape(256, 1024)
    mine = jnp.stack([tokens[:, :256], tokens[:, 256:512]])
    cot_own = cut(tokens, 512 + c * 256, 256, 1)
    cot_other = send(cut(tokens, 512 + (1 - c) * 256, 256, 1), "c", 1)
    cot = jnp.stack([cot_own, cot_other])
    partner = send(mine, "zl", 1)
    pair = jnp.stack([jnp.where(zl == 0, mine, partner), jnp.where(zl == 0, partner, mine)])
    one = send(pair, "y", 1)
    three = send(pair, "y", -1)
    two_a = send(one[:1], "y", 1)
    two_b = send(three[1:], "y", -1)
    act = jnp.concatenate([pair, three, two_a, two_b, one], axis=0).reshape(16, 256, 256)
    act_other = send(act, "c", 1)

    d_shape = jax.ShapeDtypeStruct((512, 384), BF)
    g_shape = [jax.ShapeDtypeStruct((n, 384, 256), BF) for n in (4, 4, 2, 2, 4)]
    part_shape = [jax.ShapeDtypeStruct((n, 256, 256), BF) for n in (16, 4, 4, 4, 4)]
    mark_shape = jax.ShapeDtypeStruct((8, 128), F32)
    gains = [jnp.stack([q_gain, q_gain]), jnp.stack([k_gain, k_gain])]
    scratch = [pltpu.VMEM((512, 384), F32), pltpu.VMEM((384, 512), BF)]
    arrays = (act, act_other, cot)

    def total_of(zero, back, ahead):
        return zero.astype(F32) + back.astype(F32) + ahead.astype(F32)

    def late(g, first, axis):
        n = g[2].shape[0]
        back = send(added(g[2], first[0][:n]), axis, -1)
        ahead = send(added(g[3], first[1][:n]), axis, 1)
        return back, ahead

    def finish(g, first, second):
        n = g[2].shape[0]
        from_ahead = jnp.concatenate([second[0], first[0][n:]], axis=0)
        from_behind = jnp.concatenate([first[1][n:], second[1]], axis=0)
        return total_of(g[4], from_ahead, from_behind)

    def early(g, axis):
        return send(g[0], axis, -1), send(g[1], axis, 1)

    def split_z(s):
        half = s.shape[1] // 2
        back = jnp.concatenate([s[2, :half], s[1, half:]], axis=0)
        ahead = jnp.concatenate([s[2, half:], s[3, :half]], axis=0)
        return [back, ahead, s[1, :half], s[3, half:], s[0]]

    d0, *g_0, mark = call(
        first_kernel, [d_shape, *g_shape, mark_shape], scratch, place, *arrays, *gains, weights
    )
    x_early_0 = early(g_0, "x")
    gains = tie(gains, [mark])
    part, *outs = call(
        second_kernel,
        [*part_shape, *g_shape],
        [pltpu.VMEM((512, 384), BF), *scratch],
        place,
        *arrays,
        *gains,
        weights,
        d0,
    )
    got = jnp.concatenate([send(far, "c", 1) for far in outs[:4]], axis=0)
    g_1 = outs[4:]
    x_late_0 = late(g_0, x_early_0, "x")
    on = tie([part, *g_1[:2]], x_early_0)
    part, g_1[0], g_1[1] = on
    x_early_1 = early(g_1, "x")

    part = added(part, got)
    result = lax.psum_scatter(part, ("zl", "y"), scatter_dimension=0, tiled=True)

    s_0 = split_z(finish(g_0, x_early_0, x_late_0).astype(BF))
    z_early_0 = early(s_0, "zh")
    x_late_1 = late(g_1, x_early_1, "x")

    operands = [added(s_0[2], z_early_0[0][:192]), added(s_0[3], z_early_0[1][:192])]
    operands = tie(operands, x_early_1)
    z_late_0 = (send(operands[0], "zh", -1), send(operands[1], "zh", 1))

    result = result.reshape(2, 8, 16, 2, 256).transpose(2, 1, 3, 0, 4).reshape(16, 8, 2, 512)
    result = lax.all_to_all(result, ("zh", "x"), 0, 0, tiled=True)
    grad_input = result.reshape(128, 2, 512).transpose(1, 0, 2)

    s_1 = split_z(finish(g_1, x_early_1, x_late_1).astype(BF))
    z_early_1 = early(s_1, "zh")
    z_late_1 = late(s_1, z_early_1, "zh")

    both = jnp.stack([finish(s_0, z_early_0, z_late_0), finish(s_1, z_early_1, z_late_1)])
    kept = cut(both, c * 128, 128, 2)
    (away,) = tie([cut(both, (1 - c) * 128, 128, 2).astype(BF)], [result])
    other = send(away, "c", 1).astype(F32)
    heads = jnp.concatenate([jnp.where(c == 0, kept, other), jnp.where(c == 0, other, kept)], axis=0)
    heads = heads.reshape(4, 3, 128, 128).transpose(1, 3, 0, 2).reshape(3, 128, 512)
    return (grad_input, heads[0], heads[1], heads[2])


def solution(mesh):
    fine = Mesh(mesh.devices.reshape(4, 4, 2, 2, 4), ("zh", "x", "c", "zl", "y"))
    frame = ("zh", "x", "c")
    head = ("zl", "y")
    weight = P(frame, head)
    return jax.shard_map(
        body,
        mesh=fine,
        in_specs=(P(frame, None, None), weight, weight, weight, P(), P(), P(frame, None, head)),
        out_specs=(P(frame, None, head), weight, weight, weight),
        check_vma=False,
    )
```
